32 devices in a mesh: fsdp: 4 (over y, core), tile: 8 (over z, x).
Axes of the slice: x: 2, y: 2, z: 4, core: 2. Of those that a mesh axis runs over, the one named last changes fastest.
Arguments:
- tiles: bfloat16 [4, 2048, 768], P('fsdp', 'tile')
- nbr_tiles: int32 [4, 512, 4], P('fsdp', 'tile'), may hold values from 0 to 2047, as said below
- nbr_mask: int32 [4, 512, 4], P('fsdp', 'tile'), may hold values 0 or 1
- tile_count: int32 [4], P('fsdp'), may hold values from 1024 to 2048, as said below
- w_query: bfloat16 [768, 768], P('fsdp'), may hold values from -0.21875 to 0.21875
- w_key: bfloat16 [768, 768], P('fsdp'), may hold values from -0.21875 to 0.21875
- w_value: bfloat16 [768, 768], P('fsdp'), may hold values from -0.21875 to 0.21875
- w_out: bfloat16 [768, 768], P('fsdp'), may hold values from -0.875 to 0.875
- key_gain: float32 [768], replicated, may hold values from 0.1 to 1.9
Outputs:
- attended: bfloat16 [4, 2048, 768], P('fsdp', 'tile')
The draws below stay inside these ranges and needn't reach their ends.
Inputs may be any that keep to these rules, and one draw needn't show every extreme that they name: `nbr_tiles`: the slots of region r hold tiles with indices from (r // 64 - 1) * 256 to (r // 64 + 2) * 256 - 1, within the group. `tile_count`: some group has all 2048 tiles live.
All inputs are finite; a program needn't handle non-finite values. No bound on the sum of `nbr_mask` on one device may be relied on, other than what follows from the above.
Results may differ from the reference program's by a relative error of at most 0.008.
The reference program's roundings to bfloat16 on the way (of `normed`, `weight` and `context`) count: a program that leaves them out, or rounds other values in their place, can miss the bound.
Values may be sent and summed in bfloat16 or wider, within the bound.
No kernel may reach another device: no remote copies, remote signals or barrier semaphores. Data moves between devices by JAX's collectives and lax.ppermute only.
A program may use at most 64 MiB of HBM per device.

```python
import jax
import jax.numpy as jnp
from jax import lax

D = 768
HEADS = 16
TILE_DEV = 256
NB = 4
REGIONS_PER_KEY = 8
KEY_DILATION = 2
HD = 48
GROUPS = 4
TILES = 2048
REGIONS = 512
KEYS = 64


def draw_tiles(key, part):
    base = jax.random.normal(jax.random.fold_in(key, 1), (GROUPS, TILES, D), jnp.float32)
    return base.astype(jnp.bfloat16)


def draw_nbr_tiles(key, part):
    owner = jnp.arange(REGIONS, dtype=jnp.int32) // (TILE_DEV // 4)
    offset = jax.random.randint(jax.random.fold_in(key, 5), (GROUPS, REGIONS, NB), -TILE_DEV, 2 * TILE_DEV, dtype=jnp.int32)
    return jnp.clip(owner[None, :, None] * TILE_DEV + offset, 0, TILES - 1).astype(jnp.int32)


def draw_tile_count(key, part):
    counts = jax.random.randint(jax.random.fold_in(key, 6), (GROUPS,), TILES // 2, TILES + 1, dtype=jnp.int32)
    selected_keys = jax.random.randint(jax.random.fold_in(key, 7), (), 0, GROUPS, dtype=jnp.int32)
    return jnp.where(jnp.arange(GROUPS, dtype=jnp.int32) == selected_keys, TILES, counts).astype(jnp.int32)


def with_ends(entries, key, low, top_value):
    dims = entries.shape
    place = [jax.random.randint(jax.random.fold_in(key, axis), (), 0, dims[axis]) for axis in range(len(dims))]
    entries = entries.at[tuple(place)].set(low)
    longest = dims.index(max(dims))
    place[longest] = (place[longest] + 1) % dims[longest]
    return entries.at[tuple(place)].set(top_value)


def block_scale(own_key, extent, split, smallest, top_value):
    def one(axis_at, blocks):
        steps = jax.random.uniform(jax.random.fold_in(jax.random.fold_in(own_key, 6), axis_at), (blocks,), jnp.float32, smallest / len(split), top_value / len(split))
        return jnp.repeat(jnp.exp(steps), extent[axis_at] // blocks).reshape((-1,) + (1,) * (len(extent) - axis_at - 1))

    loudness = one(*split[0])
    for cut in split[1:]:
        loudness = loudness * one(*cut)
    return loudness


def scatter_about(stream_key, extent, spread, limit, split=(), held_as=jnp.bfloat16):
    level = block_scale(stream_key, extent, split, -0.22, 0.18) if split else 1.0
    array = jax.random.normal(stream_key, extent, jnp.float32) * spread * level
    return jnp.minimum(jnp.maximum(array, -limit), limit).astype(held_as)


def setup_inputs(seed: int = 0) -> dict:
    splits = jax.random.split(jax.random.key(seed), 10)
    tiles = draw_tiles(jax.random.fold_in(splits[9], 71), 0)
    nbr_tiles = draw_nbr_tiles(jax.random.fold_in(splits[9], 71), 0)
    nbr_mask = with_ends((jax.random.randint(splits[2], (GROUPS, REGIONS, NB), 0, 4) < 3).astype(jnp.int32), jax.random.fold_in(splits[2], 1), 0, 1)
    tile_count = draw_tile_count(jax.random.fold_in(splits[9], 71), 0)
    w_query = scatter_about(splits[4], (D, D), D ** -0.5, 0.21875, ((0, 4),))
    w_key = scatter_about(splits[5], (D, D), D ** -0.5, 0.21875, ((0, 4),))
    w_value = scatter_about(splits[6], (D, D), D ** -0.5, 0.21875, ((0, 4),))
    w_out = scatter_about(splits[7], (D, D), HD ** -0.5, 0.875, ((0, 4),))
    key_gain = jnp.clip(1.0 + 0.18 * jax.random.normal(splits[8], (D,), jnp.float32), 0.1, 1.9)
    return dict(tiles=tiles, nbr_tiles=nbr_tiles, nbr_mask=nbr_mask, tile_count=tile_count, w_query=w_query, w_key=w_key, w_value=w_value, w_out=w_out, key_gain=key_gain)


def one_group(args):
    tiles, nbr_tiles, nbr_mask, key_count_total, w_query, w_key, w_value, w_out, key_gain = args
    rows = tiles.astype(jnp.float32)[nbr_tiles.reshape(-1)].reshape(REGIONS, NB, D)
    mask_f = nbr_mask.astype(jnp.float32)
    denom = jnp.maximum(lax.optimization_barrier(jnp.sum(mask_f, axis=1)), 1.0)
    region = lax.optimization_barrier(jnp.sum(rows * mask_f[:, :, None], axis=1)) / denom[:, None]
    pooled = lax.optimization_barrier(jnp.mean(region.reshape(KEYS, REGIONS_PER_KEY, D), axis=1))
    normed = (pooled * lax.rsqrt(lax.optimization_barrier(jnp.mean(pooled * pooled, axis=1, keepdims=True)) + 1e-06) * key_gain[None, :]).astype(jnp.bfloat16)
    keys = jnp.dot(normed, w_key, preferred_element_type=jnp.float32).astype(jnp.bfloat16)
    values = jnp.dot(normed, w_value, preferred_element_type=jnp.float32).astype(jnp.bfloat16)
    key_heads = keys.astype(jnp.float32).reshape(KEYS, HEADS, HD)
    value_heads = values.astype(jnp.float32).reshape(KEYS, HEADS, HD)
    key_position = jnp.arange(KEYS, dtype=jnp.int32)
    head_position = jnp.arange(HEADS, dtype=jnp.int32)
    valid_mask = ((key_position % KEY_DILATION)[None, :] == (head_position % KEY_DILATION)[:, None]) & (key_position * 4 * REGIONS_PER_KEY < key_count_total)[None, :]
    block = min(2048, TILES)

    def attend(tile_block):
        query = jnp.dot(tile_block, w_query, preferred_element_type=jnp.float32).astype(jnp.bfloat16)
        query_heads = query.astype(jnp.float32).reshape(-1, HEADS, HD)
        score = jnp.einsum('qhd,khd->hqk', query_heads, key_heads) / jnp.sqrt(jnp.float32(HD))
        score = jnp.where(valid_mask[:, None, :], score, -jnp.inf)
        top = lax.optimization_barrier(jnp.max(score, axis=2, keepdims=True))
        expo = jnp.exp(score - top)
        total = lax.optimization_barrier(jnp.sum(expo, axis=2))
        weight = expo.astype(jnp.bfloat16).astype(jnp.float32)
        context = jnp.einsum('hqk,khd->hqd', weight, value_heads) / total[:, :, None]
        context = jnp.transpose(context, (1, 0, 2)).reshape(-1, D).astype(jnp.bfloat16)
        return jnp.dot(context, w_out, preferred_element_type=jnp.float32).astype(jnp.bfloat16)
    out = lax.map(attend, tiles.reshape(TILES // block, block, D))
    return out.reshape(TILES, D)

def reference(tiles, nbr_tiles, nbr_mask, tile_count, w_query, w_key, w_value, w_out, key_gain):
    outs = []
    for group in range(GROUPS):
        outs.append(one_group((tiles[group], nbr_tiles[group], nbr_mask[group], tile_count[group], w_query, w_key, w_value, w_out, key_gain)))
    return jnp.stack(outs, axis=0)
```

```python
import functools

import jax
import jax.numpy as jnp
from jax import lax
from jax.experimental import pallas as pl
from jax.experimental.pallas import tpu as pltpu
from jax.sharding import PartitionSpec as P

HEADS = 16
NB = 4
REGIONS_PER_KEY = 8
KEY_DILATION = 2
LANE_GROUPS = 2
F32 = jnp.float32
BF16 = jnp.bfloat16


def vmem():
    return pl.BlockSpec(memory_space=pltpu.VMEM)


def smem():
    return pl.BlockSpec(memory_space=pltpu.SMEM)


def anywhere():
    return pl.BlockSpec(memory_space=pl.ANY)


def over(left, right, left_dim, right_dim, precision=None):
    return lax.dot_general(
        left,
        right,
        (((left_dim,), (right_dim,)), ((), ())),
        precision=precision,
        preferred_element_type=F32,
    )


def pool_kernel(place, slots, tiles, left, own, right):
    count, width = tiles.shape[0], slots.shape[1]
    keys = width // REGIONS_PER_KEY
    row = lax.broadcasted_iota(jnp.int32, (count, width), 0) + place[0] * count + 1
    hits = jnp.zeros((count, width), F32)
    live = jnp.zeros((1, width), F32)
    for s in range(NB):
        slot = slots[s : s + 1, :]
        hits += (slot == row).astype(F32)
        live += (slot > 0).astype(F32)
    sums = over(hits.astype(BF16), tiles[...], 0, 0)
    share = 1.0 / (jnp.maximum(live, 1.0) * REGIONS_PER_KEY)
    key = lax.broadcasted_iota(jnp.int32, (keys, width), 0)
    region = lax.broadcasted_iota(jnp.int32, (keys, width), 1)
    chosen = jnp.where(region // REGIONS_PER_KEY == key, share, 0.0)
    pooled = over(chosen, sums, 1, 0, lax.Precision.HIGHEST)
    part = keys // 3
    left[...] = pooled[:part]
    own[...] = pooled[part : 2 * part]
    right[...] = pooled[2 * part :]


def norm_kernel(own, first, second, gain, normed):
    pooled = own[...] + first[...] + second[...]
    scale = lax.rsqrt(jnp.mean(pooled * pooled, axis=1, keepdims=True) + 1e-06)
    normed[...] = (pooled * scale * gain[...]).astype(BF16)


def collect(copies, sem):
    started = []
    for n, (src, dst) in enumerate(copies):
        copy = pltpu.make_async_copy(src, dst, sem.at[n])
        copy.start()
        started.append(copy)
    return started


def rows_of(fsdp, me, own, sibling, other, far, held):
    rows = own.shape[0]
    chips = fsdp // 2
    chip, core = me // 2, me % 2

    def at(index):
        return held.at[pl.ds(pl.multiple_of(index * rows, rows), rows)]

    pieces = [(own, at(me)), (sibling, at(2 * chip + 1 - core))]
    for j in range(1, chips):
        source = lax.rem(chip - j + chips, chips)
        pieces.append((other.at[j - 1], at(2 * source + core)))
        pieces.append((far.at[j - 1], at(2 * source + 1 - core)))
    return pieces


def sorted_rows(normed):
    keys = normed.shape[0]
    half = keys // KEY_DILATION
    row = lax.broadcasted_iota(jnp.int32, (keys, keys), 0)
    column = lax.broadcasted_iota(jnp.int32, (keys, keys), 1)
    wanted = KEY_DILATION * (row % half) + row // half
    return over((column == wanted).astype(BF16), normed, 1, 0).astype(BF16)


def spread(rows, group, wide):
    half = rows.shape[0] // KEY_DILATION
    heads = HEADS // LANE_GROUPS
    size = wide // heads
    part = rows[:, group * wide : (group + 1) * wide].astype(F32)
    lane = lax.broadcasted_iota(jnp.int32, (half, wide), 1)
    out = []
    for head in range(heads):
        parity = head % KEY_DILATION
        mine = (lane >= head * size) & (lane < (head + 1) * size)
        out.append(jnp.where(mine, part[parity * half : (parity + 1) * half], 0.0))
    return jnp.concatenate(out, axis=0).astype(BF16)


def attend_scores(
    fsdp, block, place, normed, tiles, wk, wq, sibling, near, far, weights, totals, wk_held, wq_held, sem
):
    tile, me, count, pair = place[0], place[1], place[2], place[3]
    pieces = rows_of(fsdp, me, wk, sibling.at[0], near.at[pair], far.at[pair], wk_held)
    pieces += rows_of(fsdp, me, wq, sibling.at[1], near.at[1 - pair], far.at[1 - pair], wq_held)
    started = collect(pieces, sem)
    ordered = sorted_rows(normed[...])
    for copy in started:
        copy.wait()
    keys = over(ordered, wk_held[...], 1, 0).astype(BF16)
    query = over(tiles[...], wq_held[...], 1, 0).astype(BF16)
    half = keys.shape[0] // KEY_DILATION
    heads = HEADS // LANE_GROUPS
    wide = keys.shape[1] // LANE_GROUPS
    rows = tiles.shape[0]
    size = wide // heads
    row = lax.broadcasted_iota(jnp.int32, (half, 1), 0)
    per = block // KEY_DILATION
    first = (tile ^ (row // per)) * block + KEY_DILATION * (row % per)
    valid = [(first + parity) * (4 * REGIONS_PER_KEY) < count for parity in range(KEY_DILATION)]
    hidden = jnp.concatenate(
        [jnp.where(valid[head % KEY_DILATION], 0.0, -jnp.inf) for head in range(heads)], axis=0
    )
    for group in range(LANE_GROUPS):
        score = over(spread(keys, group, wide), query[:, group * wide : (group + 1) * wide], 1, 1)
        score = (score * (1.0 / size**0.5) + hidden).reshape(heads, half, rows)
        expo = jnp.exp(score - jnp.max(score, axis=1, keepdims=True))
        totals[group * heads : (group + 1) * heads, :] = jnp.sum(expo, axis=1)
        weights[group * heads * half : (group + 1) * heads * half, :] = expo.reshape(
            heads * half, rows
        ).astype(BF16)


def attend_values(
    fsdp, place, normed, weights, totals, wv, wo, sibling, near, far, out, wv_held, wo_held, sem
):
    me, pair = place[1], place[3]
    pieces = rows_of(fsdp, me, wv, sibling.at[2], near.at[pair], far.at[pair], wv_held)
    pieces += rows_of(fsdp, me, wo, sibling.at[3], near.at[1 - pair], far.at[1 - pair], wo_held)
    started = collect(pieces, sem)
    ordered = sorted_rows(normed[...])
    for copy in started:
        copy.wait()
    values = over(ordered, wv_held[...], 1, 0).astype(BF16)
    half = values.shape[0] // KEY_DILATION
    heads = HEADS // LANE_GROUPS
    wide = values.shape[1] // LANE_GROUPS
    rows = weights.shape[1]
    size = wide // heads
    total = None
    for group in range(LANE_GROUPS):
        part = weights[group * heads * half : (group + 1) * heads * half, :]
        context = over(spread(values, group, wide), part, 0, 0).reshape(heads, size, rows)
        share = 1.0 / totals[group * heads : (group + 1) * heads, :]
        context = (context * share[:, None, :]).reshape(wide, rows).astype(BF16)
        term = over(context, wo_held[group * wide : (group + 1) * wide, :], 0, 0)
        total = term if total is None else total + term
    out[...] = total.astype(BF16)


def swap(array, axis, offset):
    count = lax.axis_size(axis)
    return lax.ppermute(array, axis, [(i, i ^ offset) for i in range(count)])


def gather_rows(rows, axis):
    count = lax.axis_size(axis)
    held = 1
    digits = [1] + [2] * 16
    for digit in digits:
        if held >= count:
            break
        width = min(1 << digit, count // held)
        parts = [rows] + [swap(rows, axis, held * d) for d in range(1, width)]
        rows = jnp.concatenate(parts, axis=0)
        held *= width
    return rows


def chip_shift(array, axis, step):
    count = lax.axis_size(axis)
    return lax.ppermute(array, axis, [(i, (i + 2 * step) % count) for i in range(count)])


def fetch(first, second, pair):
    chips = lax.axis_size("fsdp") // 2
    mine = jnp.where(pair == 0, first, second)
    near = jnp.stack([chip_shift(mine, "fsdp", j) for j in range(1, chips)])
    both = jnp.stack([near, swap(near, "tile", 1)])
    return both, swap(both, "fsdp", 1)


def body(tiles, nbr_tiles, nbr_mask, tile_count, w_query, w_key, w_value, w_out, key_gain):
    own_tiles = tiles[0]
    rows, width = own_tiles.shape
    tile = lax.axis_index("tile")
    me = lax.axis_index("fsdp")
    tile_devices = lax.axis_size("tile")
    fsdp = lax.axis_size("fsdp")
    regions = nbr_tiles.shape[1]
    block = regions // REGIONS_PER_KEY
    place = jnp.stack([tile, me, tile_count[0], tile % 2]).astype(jnp.int32)

    forward = [(i, i + 1) for i in range(tile_devices - 1)]
    backward = [(i + 1, i) for i in range(tile_devices - 1)]
    slots = jnp.where(nbr_mask[0] > 0, nbr_tiles[0] + 1, 0).T
    slots_all = jnp.concatenate(
        [lax.ppermute(slots, "tile", forward), slots, lax.ppermute(slots, "tile", backward)], axis=1
    )
    part = jax.ShapeDtypeStruct((block, width), F32)
    left, own, right = pl.pallas_call(
        pool_kernel,
        out_shape=(part, part, part),
        in_specs=[smem(), vmem(), vmem()],
        out_specs=(vmem(), vmem(), vmem()),
        name="pool",
    )(place, slots_all, own_tiles)
    normed = pl.pallas_call(
        norm_kernel,
        out_shape=jax.ShapeDtypeStruct((block, width), BF16),
        in_specs=[vmem()] * 4,
        out_specs=vmem(),
        name="norm",
    )(
        own,
        lax.ppermute(right, "tile", forward),
        lax.ppermute(left, "tile", backward),
        key_gain[None, :],
    )
    normed = gather_rows(normed, "tile")
    keys = normed.shape[0]

    sibling = swap(jnp.stack([w_key, w_query, w_value, w_out]), "fsdp", 1)
    near1, far1 = fetch(w_key, w_query, tile % 2)
    near2, far2 = fetch(w_value, w_out, tile % 2)

    held = pltpu.VMEM((width, width), BF16)
    scratch = [held, held, pltpu.SemaphoreType.DMA((2 * fsdp,))]
    limit = pltpu.CompilerParams(vmem_limit_bytes=40 * 1024 * 1024)
    weights, totals = pl.pallas_call(
        functools.partial(attend_scores, fsdp, block),
        out_shape=(
            jax.ShapeDtypeStruct((HEADS * keys // KEY_DILATION, rows), BF16),
            jax.ShapeDtypeStruct((HEADS, rows), F32),
        ),
        in_specs=[smem(), vmem(), vmem()] + [anywhere()] * 5,
        out_specs=(vmem(), vmem()),
        scratch_shapes=scratch,
        compiler_params=limit,
        name="scores",
    )(place, normed, own_tiles, w_key, w_query, sibling, near1, far1)
    attended = pl.pallas_call(
        functools.partial(attend_values, fsdp),
        out_shape=jax.ShapeDtypeStruct((rows, width), BF16),
        in_specs=[smem()] + [vmem()] * 3 + [anywhere()] * 5,
        out_specs=vmem(),
        scratch_shapes=scratch,
        compiler_params=limit,
        name="values",
    )(place, normed, weights, totals, w_value, w_out, sibling, near2, far2)
    return attended[None]


def solution(mesh):
    placed = (
        P("fsdp", "tile", None),
        P("fsdp", "tile", None),
        P("fsdp", "tile", None),
        P("fsdp"),
        P("fsdp", None),
        P("fsdp", None),
        P("fsdp", None),
        P("fsdp", None),
        P(),
    )
    return jax.shard_map(
        body, mesh=mesh, in_specs=placed, out_specs=P("fsdp", "tile", None), check_vma=False
    )
```

```python
import functools

import jax
import jax.numpy as jnp
from jax import lax
from jax.experimental import pallas as pl
from jax.experimental.pallas import tpu as pltpu
from jax.sharding import PartitionSpec as P

HEADS = 16
NB = 4
REGIONS_PER_KEY = 8
KEY_DILATION = 2
LANE_GROUPS = 2
F32 = jnp.float32
BF16 = jnp.bfloat16


def vmem():
    return pl.BlockSpec(memory_space=pltpu.VMEM)


def smem():
    return pl.BlockSpec(memory_space=pltpu.SMEM)


def anywhere():
    return pl.BlockSpec(memory_space=pl.ANY)


def over(left, right, left_dim, right_dim, precision=None):
    return lax.dot_general(
        left,
        right,
        (((left_dim,), (right_dim,)), ((), ())),
        precision=precision,
        preferred_element_type=F32,
    )


def pool_kernel(before, here, after, tiles, left, own, right):
    count = tiles.shape[0]
    regions = here.shape[0]
    base = lax.axis_index("tile") * count + 1
    row = lax.broadcasted_iota(jnp.int32, (regions, count), 1) + base
    hits, shares = [], []
    for slots in (before, here, after):
        hit = jnp.zeros((regions, count), F32)
        live = jnp.zeros((regions, 1), F32)
        for s in range(NB):
            slot = slots[:, s : s + 1]
            hit += (slot == row).astype(F32)
            live += (slot > 0).astype(F32)
        hits.append(hit.astype(BF16))
        shares.append(1.0 / (jnp.maximum(live, 1.0) * REGIONS_PER_KEY))
    sums = over(jnp.concatenate(hits, axis=0), tiles[...], 1, 0)
    sums = sums * jnp.concatenate(shares, axis=0)
    pooled = jnp.sum(sums.reshape(-1, REGIONS_PER_KEY, sums.shape[1]), axis=1)
    part = regions // REGIONS_PER_KEY
    left[...] = pooled[:part]
    own[...] = pooled[part : 2 * part]
    right[...] = pooled[2 * part :]


def collect(copies, sem):
    started = []
    for n, (src, dst) in enumerate(copies):
        copy = pltpu.make_async_copy(src, dst, sem.at[n])
        copy.start()
        started.append(copy)
    return started


def piece_rows(fsdp, rows):
    me = lax.axis_index("fsdp")
    chips = fsdp // 2
    chip, core = me // 2, me % 2
    owners = [me, 2 * chip + 1 - core]
    for j in range(1, chips):
        source = lax.rem(chip - j + chips, chips)
        owners += [2 * source + core, 2 * source + 1 - core]
    return [pl.multiple_of(owner * rows, rows) for owner in owners]


def sorted_rows(normed):
    keys = normed.shape[0]
    half = keys // KEY_DILATION
    row = lax.broadcasted_iota(jnp.int32, (keys, keys), 0)
    column = lax.broadcasted_iota(jnp.int32, (keys, keys), 1)
    wanted = KEY_DILATION * (row % half) + row // half
    return over((column == wanted).astype(BF16), normed, 1, 0).astype(BF16)


def spread(rows, group, wide):
    half = rows.shape[0] // KEY_DILATION
    heads = HEADS // LANE_GROUPS
    size = wide // heads
    part = rows[:, group * wide : (group + 1) * wide].astype(F32)
    lane = lax.broadcasted_iota(jnp.int32, (half, wide), 1)
    out = []
    for head in range(heads):
        parity = head % KEY_DILATION
        mine = (lane >= head * size) & (lane < (head + 1) * size)
        out.append(jnp.where(mine, part[parity * half : (parity + 1) * half], 0.0))
    return jnp.concatenate(out, axis=0).astype(BF16)


def attend_kernel(fsdp, block, *refs):
    count, normed, tiles = refs[:3]
    pieces = refs[3 : 3 + 3 * fsdp]
    out, held, sem = refs[3 + 3 * fsdp :]
    shard = pieces[0].shape[0]
    begins = piece_rows(fsdp, shard)
    copies = [
        (pieces[w * fsdp + i], held.at[w, pl.ds(begins[i], shard)])
        for w in range(3)
        for i in range(fsdp)
    ]
    started = collect(copies, sem)
    ordered = sorted_rows(normed[...])
    for copy in started:
        copy.wait()
    query = over(tiles[...], held[0], 1, 0).astype(BF16)
    keys = over(ordered, held[1], 1, 0).astype(BF16)
    values = over(ordered, held[2], 1, 0).astype(BF16)
    half = keys.shape[0] // KEY_DILATION
    heads = HEADS // LANE_GROUPS
    wide = keys.shape[1] // LANE_GROUPS
    rows = tiles.shape[0]
    size = wide // heads
    row = lax.broadcasted_iota(jnp.int32, (half, 1), 0)
    valid = [
        (KEY_DILATION * row + parity) * (4 * REGIONS_PER_KEY) < count[0]
        for parity in range(KEY_DILATION)
    ]
    hidden = jnp.concatenate(
        [jnp.where(valid[head % KEY_DILATION], 0.0, -jnp.inf) for head in range(heads)], axis=0
    )
    for group in range(LANE_GROUPS):
        lanes = slice(group * wide, (group + 1) * wide)
        score = over(spread(keys, group, wide), query[:, lanes], 1, 1)
        score = (score * (1.0 / size**0.5) + hidden).reshape(heads, half, rows)
        expo = jnp.exp(score - jnp.max(score, axis=1, keepdims=True))
        share = 1.0 / jnp.sum(expo, axis=1, keepdims=True)
        weight = expo.reshape(heads * half, rows).astype(BF16)
        context = over(spread(values, group, wide), weight, 0, 0).reshape(heads, size, rows)
        out[lanes, :] = (context * share).reshape(wide, rows).astype(BF16)


def project_kernel(fsdp, first, count, last, *refs):
    context = refs[0]
    before = None if first == 0 else refs[1]
    pieces = refs[-1 - count : -1]
    out = refs[-1]
    shard = pieces[0].shape[0]
    begins = piece_rows(fsdp, shard)
    total = None if before is None else before[...]
    for i, piece in enumerate(pieces):
        part = over(context[pl.ds(begins[first + i], shard), :], piece[...], 0, 0)
        total = part if total is None else total + part
    out[...] = total.astype(out.dtype)


def swap(array, axis, offset):
    count = lax.axis_size(axis)
    return lax.ppermute(array, axis, [(i, i ^ offset) for i in range(count)])


def chip_shift(array, axis, step):
    count = lax.axis_size(axis)
    return lax.ppermute(array, axis, [(i, (i + 2 * step) % count) for i in range(count)])


def gather_weight(weight):
    chips = lax.axis_size("fsdp") // 2
    pieces = [weight, swap(weight, "fsdp", 1)]
    for j in range(1, chips):
        near = chip_shift(weight, "fsdp", j)
        pieces += [near, swap(near, "fsdp", 1)]
    return pieces


def body(tiles, nbr_tiles, nbr_mask, tile_count, w_query, w_key, w_value, w_out, key_gain):
    own_tiles = tiles[0]
    rows, width = own_tiles.shape
    tile_devices = lax.axis_size("tile")
    fsdp = lax.axis_size("fsdp")
    regions = nbr_tiles.shape[1]
    block = regions // REGIONS_PER_KEY

    forward = [(i, i + 1) for i in range(tile_devices - 1)]
    backward = [(i + 1, i) for i in range(tile_devices - 1)]
    slots = jnp.where(nbr_mask[0] > 0, nbr_tiles[0] + 1, 0)
    before = lax.ppermute(slots, "tile", forward)
    after = lax.ppermute(slots, "tile", backward)
    part = jax.ShapeDtypeStruct((block, width), F32)
    left, own, right = pl.pallas_call(
        pool_kernel,
        out_shape=(part, part, part),
        in_specs=[vmem()] * 4,
        out_specs=(vmem(), vmem(), vmem()),
        name="pool",
    )(before, slots, after, own_tiles)
    pooled = (
        own + lax.ppermute(right, "tile", forward) + lax.ppermute(left, "tile", backward)
    )
    scale = lax.rsqrt(jnp.mean(pooled * pooled, axis=1, keepdims=True) + 1e-06)
    normed = (pooled * scale * key_gain[None, :]).astype(BF16)
    normed = lax.all_to_all(
        jnp.tile(normed, (tile_devices, 1)), "tile", split_axis=0, concat_axis=0, tiled=True
    )

    keys = gather_weight(w_key)
    values = gather_weight(w_value)
    queries = gather_weight(w_query)
    outs = gather_weight(w_out)

    limit = pltpu.CompilerParams(vmem_limit_bytes=40 * 1024 * 1024)
    context = pl.pallas_call(
        functools.partial(attend_kernel, fsdp, block),
        out_shape=jax.ShapeDtypeStruct((width, rows), BF16),
        in_specs=[smem(), vmem(), vmem()] + [anywhere()] * (3 * fsdp),
        out_specs=vmem(),
        scratch_shapes=[
            pltpu.VMEM((3, width, width), BF16),
            pltpu.SemaphoreType.DMA((3 * fsdp,)),
        ],
        compiler_params=limit,
        name="attend",
    )(tile_count, normed, own_tiles, *queries, *keys, *values)
    partial = pl.pallas_call(
        functools.partial(project_kernel, fsdp, 0, 2, False),
        out_shape=jax.ShapeDtypeStruct((rows, width), F32),
        in_specs=[vmem()] * 3,
        out_specs=vmem(),
        compiler_params=limit,
        name="project_near",
    )(context, *outs[:2])
    attended = pl.pallas_call(
        functools.partial(project_kernel, fsdp, 2, fsdp - 2, True),
        out_shape=jax.ShapeDtypeStruct((rows, width), BF16),
        in_specs=[vmem()] * fsdp,
        out_specs=vmem(),
        compiler_params=limit,
        name="project_far",
    )(context, partial, *outs[2:])
    return attended[None]


def solution(mesh):
    placed = (
        P("fsdp", "tile", None),
        P("fsdp", "tile", None),
        P("fsdp", "tile", None),
        P("fsdp"),
        P("fsdp", None),
        P("fsdp", None),
        P("fsdp", None),
        P("fsdp", None),
        P(),
    )
    return jax.shard_map(
        body, mesh=mesh, in_specs=placed, out_specs=P("fsdp", "tile", None), check_vma=False
    )
```

```python
import functools

import jax
import jax.numpy as jnp
from jax import lax
from jax.experimental import pallas as pl
from jax.experimental.pallas import tpu as pltpu
from jax.sharding import PartitionSpec as P

HEADS = 16
NB = 4
REGIONS_PER_KEY = 8
KEY_DILATION = 2
LANE_GROUPS = 2
F32 = jnp.float32
BF16 = jnp.bfloat16


def vmem():
    return pl.BlockSpec(memory_space=pltpu.VMEM)


def smem():
    return pl.BlockSpec(memory_space=pltpu.SMEM)


def anywhere():
    return pl.BlockSpec(memory_space=pl.ANY)


def over(left, right, left_dim, right_dim, precision=None):
    return lax.dot_general(
        left,
        right,
        (((left_dim,), (right_dim,)), ((), ())),
        precision=precision,
        preferred_element_type=F32,
    )


def pool_kernel(here, mate, other, tiles, out):
    count = tiles.shape[0]
    regions = here.shape[0]
    base = lax.axis_index("tile") * count + 1
    row = lax.broadcasted_iota(jnp.int32, (regions, count), 1) + base
    hits, shares = [], []
    for slots in (here, mate, other):
        hit = jnp.zeros((regions, count), F32)
        live = jnp.zeros((regions, 1), F32)
        for s in range(NB):
            slot = slots[:, s : s + 1]
            hit += (slot == row).astype(F32)
            live += (slot > 0).astype(F32)
        hits.append(hit.astype(BF16))
        shares.append(1.0 / (jnp.maximum(live, 1.0) * REGIONS_PER_KEY))
    sums = over(jnp.concatenate(hits, axis=0), tiles[...], 1, 0)
    sums = sums * jnp.concatenate(shares, axis=0)
    out[...] = jnp.sum(sums.reshape(-1, REGIONS_PER_KEY, sums.shape[1]), axis=1)


def pair_kernel(mine, theirs, out):
    block = mine.shape[0] // 3
    first = mine[:block] + theirs[block : 2 * block]
    second = mine[block : 2 * block] + theirs[:block]
    inner = jnp.concatenate([first, second], axis=0)
    high = inner.astype(BF16)
    out[: 2 * block, :] = high
    out[2 * block : 4 * block, :] = (inner - high.astype(F32)).astype(BF16)
    outer = jnp.concatenate([mine[2 * block :], theirs[2 * block :]], axis=0)
    out[4 * block :, :] = outer.astype(BF16)


def collect(copies, sem):
    started = []
    for n, (src, dst) in enumerate(copies):
        copy = pltpu.make_async_copy(src, dst, sem.at[n])
        copy.start()
        started.append(copy)
    return started


def sorted_rows(normed):
    keys = normed.shape[0]
    half = keys // KEY_DILATION
    row = lax.broadcasted_iota(jnp.int32, (keys, keys), 0)
    column = lax.broadcasted_iota(jnp.int32, (keys, keys), 1)
    wanted = KEY_DILATION * (row % half) + row // half
    return over((column == wanted).astype(BF16), normed, 1, 0).astype(BF16)


def spread(rows, group, wide):
    half = rows.shape[0] // KEY_DILATION
    heads = HEADS // LANE_GROUPS
    size = wide // heads
    part = rows[:, group * wide : (group + 1) * wide].astype(F32)
    lane = lax.broadcasted_iota(jnp.int32, (half, wide), 1)
    out = []
    for head in range(heads):
        parity = head % KEY_DILATION
        mine = (lane >= head * size) & (lane < (head + 1) * size)
        out.append(jnp.where(mine, part[parity * half : (parity + 1) * half], 0.0))
    return jnp.concatenate(out, axis=0).astype(BF16)


def attend_kernel(fsdp, block, *refs):
    count, sums, gain, tiles = refs[:4]
    own, mate = refs[4:8], refs[8]
    near, far = refs[9:12], refs[12:15]
    out, held, pooled, sem = refs[15:]
    shard = mate.shape[1]
    chips = fsdp // 2
    half_width = held.shape[2] // 2
    device = lax.axis_index("tile")
    me = lax.axis_index("fsdp")
    chip, core = me // 2, me % 2
    cut = device % 2

    def at(weight, owner, side=None):
        rows = pl.ds(pl.multiple_of(owner * shard, shard), shard)
        if side is None:
            return held.at[weight, rows]
        columns = pl.ds(pl.multiple_of(side * half_width, half_width), half_width)
        return held.at[weight, rows, columns]

    copies = []
    for weight in range(4):
        copies.append((own[weight], at(weight, me)))
        copies.append((mate.at[weight], at(weight, 2 * chip + 1 - core)))
        for j in range(1, chips):
            source = 2 * lax.rem(chip - j + chips, chips)
            for pieces, owner in ((near, source + core), (far, source + 1 - core)):
                whole, mine, theirs = pieces
                if weight < 2:
                    copies.append((whole.at[j - 1, weight], at(weight, owner)))
                else:
                    copies.append((mine.at[j - 1, weight - 2], at(weight, owner, cut)))
                    copies.append((theirs.at[j - 1, weight - 2], at(weight, owner, 1 - cut)))
    started = collect(copies, sem)
    counts = [fsdp, fsdp, 2 + 4 * (chips - 1), 2 + 4 * (chips - 1)]

    def arrive(weight):
        begin = sum(counts[:weight])
        for copy in started[begin : begin + counts[weight]]:
            copy.wait()

    pooled[...] = jnp.zeros_like(pooled)
    pairs = sums.shape[0] // (6 * block)
    for s in range(pairs):
        even = device ^ (2 * s)
        odd = even ^ 1
        blocks = [even, odd, even, odd, even - 1 + 2 * (even % 2), odd - 1 + 2 * (odd % 2)]
        for i, index in enumerate(blocks):
            begin = (6 * s + i) * block
            rows = pl.ds(pl.multiple_of((index + 1) * block, block), block)
            pooled[rows, :] += sums[begin : begin + block, :].astype(F32)
    mean = pooled[block : (2 * pairs + 1) * block, :]
    scale = lax.rsqrt(jnp.mean(mean * mean, axis=1, keepdims=True) + 1e-06)
    normed = (mean * scale * gain[...]).astype(BF16)
    ordered = sorted_rows(normed)
    arrive(0)
    query = over(tiles[...], held[0], 1, 0).astype(BF16)
    arrive(1)
    keys = over(ordered, held[1], 1, 0).astype(BF16)
    arrive(2)
    values = over(ordered, held[2], 1, 0).astype(BF16)
    half = keys.shape[0] // KEY_DILATION
    heads = HEADS // LANE_GROUPS
    wide = keys.shape[1] // LANE_GROUPS
    rows = tiles.shape[0]
    size = wide // heads
    row = lax.broadcasted_iota(jnp.int32, (half, 1), 0)
    valid = [
        (KEY_DILATION * row + parity) * (4 * REGIONS_PER_KEY) < count[0]
        for parity in range(KEY_DILATION)
    ]
    hidden = jnp.concatenate(
        [jnp.where(valid[head % KEY_DILATION], 0.0, -jnp.inf) for head in range(heads)], axis=0
    )
    contexts = []
    for group in range(LANE_GROUPS):
        lanes = slice(group * wide, (group + 1) * wide)
        score = over(spread(keys, group, wide), query[:, lanes], 1, 1)
        score = (score * (1.0 / size**0.5) + hidden).reshape(heads, half, rows)
        expo = jnp.exp(score - jnp.max(score, axis=1, keepdims=True))
        share = 1.0 / jnp.sum(expo, axis=1, keepdims=True)
        weight = expo.reshape(heads * half, rows).astype(BF16)
        context = over(spread(values, group, wide), weight, 0, 0).reshape(heads, size, rows)
        contexts.append((context * share).reshape(wide, rows).astype(BF16))
    arrive(3)
    context = jnp.concatenate(contexts, axis=0)
    out[...] = over(context, held[3], 0, 0).astype(out.dtype)


def swap(array, axis, offset):
    count = lax.axis_size(axis)
    return lax.ppermute(array, axis, [(i, i ^ offset) for i in range(count)])


def chip_shift(array, axis, step):
    count = lax.axis_size(axis)
    return lax.ppermute(array, axis, [(i, (i + 2 * step) % count) for i in range(count)])


def stack_kernel(w_query, w_key, w_value, w_out, halves, pair, whole, sem):
    cut = lax.axis_index("tile") % 2
    width = halves.shape[2]
    columns = pl.ds(pl.multiple_of(cut * width, width), width)
    copies = [(w.at[:, columns], halves.at[n]) for n, w in enumerate((w_value, w_out))]
    copies += [(w, pair.at[n]) for n, w in enumerate((w_query, w_key))]
    copies += [(w, whole.at[n]) for n, w in enumerate((w_query, w_key, w_value, w_out))]
    for copy in collect(copies, sem):
        copy.wait()


def behind(array, *others):
    return lax.optimization_barrier((array,) + others)[0]


def from_chips(weight):
    chips = lax.axis_size("fsdp") // 2
    return jnp.stack([chip_shift(weight, "fsdp", j) for j in range(1, chips)])


def gather_pairs(rows, axis):
    pairs = lax.axis_size(axis) // 2
    held = 1
    while held < pairs:
        width = min(4, pairs // held)
        parts = [rows] + [swap(rows, axis, 2 * held * d) for d in range(1, width)]
        rows = jnp.concatenate(parts, axis=0)
        held *= width
    return rows


def local_call(kernel, out_shape, in_specs, name, scratch=()):
    return pl.pallas_call(
        kernel,
        out_shape=out_shape,
        in_specs=in_specs,
        out_specs=vmem(),
        scratch_shapes=list(scratch),
        compiler_params=pltpu.CompilerParams(vmem_limit_bytes=40 * 1024 * 1024),
        cost_estimate=pl.CostEstimate(flops=1000, bytes_accessed=1000, transcendentals=0),
        name=name,
    )


def body(tiles, nbr_tiles, nbr_mask, tile_count, w_query, w_key, w_value, w_out, key_gain):
    own_tiles = tiles[0]
    rows, width = own_tiles.shape
    tile_devices = lax.axis_size("tile")
    fsdp = lax.axis_size("fsdp")
    regions = nbr_tiles.shape[1]
    block = regions // REGIONS_PER_KEY

    shard = w_query.shape[0]
    halves, first_two, whole = pl.pallas_call(
        stack_kernel,
        out_shape=(
            jax.ShapeDtypeStruct((2, shard, width // 2), BF16),
            jax.ShapeDtypeStruct((2, shard, width), BF16),
            jax.ShapeDtypeStruct((4, shard, width), BF16),
        ),
        in_specs=[anywhere()] * 4,
        out_specs=(vmem(), vmem(), vmem()),
        scratch_shapes=[pltpu.SemaphoreType.DMA((8,))],
        name="stack",
    )(w_query, w_key, w_value, w_out)
    near_halves = from_chips(halves)
    near_two = from_chips(first_two)
    mate_whole = swap(whole, "fsdp", 1)

    slots = jnp.where(nbr_mask[0] > 0, nbr_tiles[0] + 1, 0)
    mate = swap(slots, "tile", 1)
    inner = [(i, i + 1) for i in range(1, tile_devices - 1, 2)]
    other = lax.ppermute(slots, "tile", inner + [(b, a) for a, b in inner])
    mine = local_call(
        pool_kernel,
        jax.ShapeDtypeStruct((3 * block, width), F32),
        [vmem()] * 4,
        "pool",
    )(slots, mate, other, behind(own_tiles, mate_whole))
    pair = local_call(
        pair_kernel,
        jax.ShapeDtypeStruct((6 * block, width), BF16),
        [vmem()] * 2,
        "pair",
    )(mine, swap(mine, "tile", 1))
    near_halves = behind(near_halves, pair)
    other_halves = swap(near_halves, "tile", 1)
    far_halves = swap(near_halves, "fsdp", 1)
    sums = gather_pairs(pair, "tile")
    near_two = behind(near_two, sums)
    other_halves = behind(other_halves, sums)
    far_two = swap(near_two, "fsdp", 1)
    far_other = swap(other_halves, "fsdp", 1)
    chips = fsdp // 2
    attended = local_call(
        functools.partial(attend_kernel, fsdp, block),
        jax.ShapeDtypeStruct((rows, width), BF16),
        [smem()] + [vmem()] * 3 + [anywhere()] * 11,
        "attend",
        [
            pltpu.VMEM((4, width, width), BF16),
            pltpu.VMEM(((tile_devices + 2) * block, width), F32),
            pltpu.SemaphoreType.DMA((2 * fsdp + 2 * (2 + 4 * (chips - 1)),)),
        ],
    )(
        tile_count,
        sums,
        key_gain[None, :],
        own_tiles,
        *(w_query, w_key, w_value, w_out),
        mate_whole,
        *(near_two, near_halves, other_halves),
        *(far_two, far_halves, far_other),
    )
    return attended[None]


def solution(mesh):
    placed = (
        P("fsdp", "tile", None),
        P("fsdp", "tile", None),
        P("fsdp", "tile", None),
        P("fsdp"),
        P("fsdp", None),
        P("fsdp", None),
        P("fsdp", None),
        P("fsdp", None),
        P(),
    )
    return jax.shard_map(
        body, mesh=mesh, in_specs=placed, out_specs=P("fsdp", "tile", None), check_vma=False
    )
```

```python
import functools

import jax
import jax.numpy as jnp
from jax import lax
from jax.experimental import pallas as pl
from jax.experimental.pallas import tpu as pltpu
from jax.sharding import PartitionSpec as P

HEADS = 16
NB = 4
REGIONS_PER_KEY = 8
KEY_DILATION = 2
LANE_GROUPS = 2
F32 = jnp.float32
BF16 = jnp.bfloat16


def vmem():
    return pl.BlockSpec(memory_space=pltpu.VMEM)


def smem():
    return pl.BlockSpec(memory_space=pltpu.SMEM)


def anywhere():
    return pl.BlockSpec(memory_space=pl.ANY)


def over(left, right, left_dim, right_dim, precision=None):
    return lax.dot_general(
        left,
        right,
        (((left_dim,), (right_dim,)), ((), ())),
        precision=precision,
        preferred_element_type=F32,
    )


def pool_kernel(here, mate, other, tiles, out):
    count = tiles.shape[0]
    regions = here.shape[0]
    base = lax.axis_index("tile") * count + 1
    row = lax.broadcasted_iota(jnp.int32, (regions, count), 1) + base
    hits, shares = [], []
    for slots in (here, mate, other):
        hit = jnp.zeros((regions, count), F32)
        live = jnp.zeros((regions, 1), F32)
        for s in range(NB):
            slot = slots[:, s : s + 1]
            hit += (slot == row).astype(F32)
            live += (slot > 0).astype(F32)
        hits.append(hit.astype(BF16))
        shares.append(1.0 / (jnp.maximum(live, 1.0) * REGIONS_PER_KEY))
    sums = over(jnp.concatenate(hits, axis=0), tiles[...], 1, 0)
    sums = sums * jnp.concatenate(shares, axis=0)
    out[...] = jnp.sum(sums.reshape(-1, REGIONS_PER_KEY, sums.shape[1]), axis=1)


def pair_kernel(mine, theirs, out):
    block = mine.shape[0] // 3
    first = mine[:block] + theirs[block : 2 * block]
    second = mine[block : 2 * block] + theirs[:block]
    inner = jnp.concatenate([first, second], axis=0)
    high = inner.astype(BF16)
    out[: 2 * block, :] = high
    out[2 * block : 4 * block, :] = (inner - high.astype(F32)).astype(BF16)
    outer = jnp.concatenate([mine[2 * block :], theirs[2 * block :]], axis=0)
    out[4 * block :, :] = outer.astype(BF16)


def collect(copies, sem):
    started = []
    for n, (src, dst) in enumerate(copies):
        copy = pltpu.make_async_copy(src, dst, sem.at[n])
        copy.start()
        started.append(copy)
    return started


def sorted_rows(normed):
    keys = normed.shape[0]
    half = keys // KEY_DILATION
    row = lax.broadcasted_iota(jnp.int32, (keys, keys), 0)
    column = lax.broadcasted_iota(jnp.int32, (keys, keys), 1)
    wanted = KEY_DILATION * (row % half) + row // half
    return over((column == wanted).astype(BF16), normed, 1, 0).astype(BF16)


def spread(rows, group, wide):
    half = rows.shape[0] // KEY_DILATION
    heads = HEADS // LANE_GROUPS
    size = wide // heads
    part = rows[:, group * wide : (group + 1) * wide].astype(F32)
    lane = lax.broadcasted_iota(jnp.int32, (half, wide), 1)
    out = []
    for head in range(heads):
        parity = head % KEY_DILATION
        mine = (lane >= head * size) & (lane < (head + 1) * size)
        out.append(jnp.where(mine, part[parity * half : (parity + 1) * half], 0.0))
    return jnp.concatenate(out, axis=0).astype(BF16)


def place_rows(fsdp, shard, held):
    half_width = held.shape[2] // 2
    chips = fsdp // 2
    me = lax.axis_index("fsdp")
    cut = lax.axis_index("tile") % 2
    chip, core = me // 2, me % 2

    def at(weight, owner, side):
        rows = pl.ds(pl.multiple_of(owner * shard, shard), shard)
        if side is None:
            return held.at[weight, rows]
        columns = pl.ds(pl.multiple_of(side * half_width, half_width), half_width)
        return held.at[weight, rows, columns]

    def own(weight, piece, mate):
        return [(piece, at(weight, me, None)), (mate, at(weight, 2 * chip + 1 - core, None))]

    def others(weight, near, far, side=None):
        copies = []
        for j in range(1, chips):
            source = 2 * lax.rem(chip - j + chips, chips)
            columns = None if side is None else (cut if side == 0 else 1 - cut)
            copies.append((near(j - 1), at(weight, source + core, columns)))
            copies.append((far(j - 1), at(weight, source + 1 - core, columns)))
        return copies

    return own, others


def query_kernel(fsdp, tiles, piece, mate, near, far, out, held, sem):
    own, others = place_rows(fsdp, piece.shape[0], held)
    copies = own(0, piece, mate) + others(0, lambda j: near.at[j], lambda j: far.at[j])
    for copy in collect(copies, sem):
        copy.wait()
    out[...] = over(tiles[...], held[0], 1, 0).astype(BF16)


def attend_kernel(fsdp, block, *refs):
    count, sums, gain, query = refs[:4]
    pieces, mates = refs[4:7], refs[7:10]
    near, far = refs[10:13], refs[13:16]
    out, held, pooled, sem = refs[16:]
    device = lax.axis_index("tile")
    own, others = place_rows(fsdp, pieces[0].shape[0], held)
    copies, ends = [], []
    for weight in (1, 2, 0):
        copies += own(weight, pieces[weight], mates[weight])
        if weight == 0:
            copies += others(0, lambda j: near[0].at[j], lambda j: far[0].at[j])
        else:
            for side in range(2):
                copies += others(
                    weight,
                    lambda j: near[1 + side].at[j, weight - 1],
                    lambda j: far[1 + side].at[j, weight - 1],
                    side,
                )
        ends.append(len(copies))
    started = collect(copies, sem)

    def arrive(begin, end):
        for copy in started[begin:end]:
            copy.wait()

    pooled[...] = jnp.zeros_like(pooled)
    pairs = sums.shape[0] // (6 * block)
    for s in range(pairs):
        even = device ^ (2 * s)
        odd = even ^ 1
        blocks = [even, odd, even, odd, even - 1 + 2 * (even % 2), odd - 1 + 2 * (odd % 2)]
        for i, index in enumerate(blocks):
            begin = (6 * s + i) * block
            rows = pl.ds(pl.multiple_of((index + 1) * block, block), block)
            pooled[rows, :] += sums[begin : begin + block, :].astype(F32)
    mean = pooled[block : (2 * pairs + 1) * block, :]
    scale = lax.rsqrt(jnp.mean(mean * mean, axis=1, keepdims=True) + 1e-06)
    normed = (mean * scale * gain[...]).astype(BF16)
    ordered = sorted_rows(normed)
    arrive(0, ends[0])
    values = over(ordered, held[1], 1, 0).astype(BF16)
    arrive(ends[1], ends[2])
    keys = over(ordered, held[0], 1, 0).astype(BF16)
    half = keys.shape[0] // KEY_DILATION
    heads = HEADS // LANE_GROUPS
    wide = keys.shape[1] // LANE_GROUPS
    rows = query.shape[0]
    size = wide // heads
    row = lax.broadcasted_iota(jnp.int32, (half, 1), 0)
    valid = [
        (KEY_DILATION * row + parity) * (4 * REGIONS_PER_KEY) < count[0]
        for parity in range(KEY_DILATION)
    ]
    hidden = jnp.concatenate(
        [jnp.where(valid[head % KEY_DILATION], 0.0, -jnp.inf) for head in range(heads)], axis=0
    )
    contexts = []
    for group in range(LANE_GROUPS):
        lanes = slice(group * wide, (group + 1) * wide)
        score = over(spread(keys, group, wide), query[:, lanes], 1, 1)
        score = (score * (1.0 / size**0.5) + hidden).reshape(heads, half, rows)
        expo = jnp.exp(score - jnp.max(score, axis=1, keepdims=True))
        share = 1.0 / jnp.sum(expo, axis=1, keepdims=True)
        weight = expo.reshape(heads * half, rows).astype(BF16)
        context = over(spread(values, group, wide), weight, 0, 0).reshape(heads, size, rows)
        contexts.append((context * share).reshape(wide, rows).astype(BF16))
    arrive(ends[0], ends[1])
    context = jnp.concatenate(contexts, axis=0)
    out[...] = over(context, held[2], 0, 0).astype(out.dtype)


def swap(array, axis, offset):
    count = lax.axis_size(axis)
    return lax.ppermute(array, axis, [(i, i ^ offset) for i in range(count)])


def chip_shift(array, axis, step):
    count = lax.axis_size(axis)
    return lax.ppermute(array, axis, [(i, (i + 2 * step) % count) for i in range(count)])


def halves_kernel(w_value, w_out, halves, sem):
    cut = lax.axis_index("tile") % 2
    width = halves.shape[2]
    columns = pl.ds(pl.multiple_of(cut * width, width), width)
    copies = [(w.at[:, columns], halves.at[n]) for n, w in enumerate((w_value, w_out))]
    for copy in collect(copies, sem):
        copy.wait()


def behind(array, *others):
    return lax.optimization_barrier((array,) + others)[0]


def from_chips(weight):
    chips = lax.axis_size("fsdp") // 2
    return jnp.stack([chip_shift(weight, "fsdp", j) for j in range(1, chips)])


def gather_pairs(rows, axis):
    pairs = lax.axis_size(axis) // 2
    held = 1
    while held < pairs:
        width = min(4, pairs // held)
        parts = [rows] + [swap(rows, axis, 2 * held * d) for d in range(1, width)]
        rows = jnp.concatenate(parts, axis=0)
        held *= width
    return rows


def local_call(kernel, out_shape, in_specs, name, scratch=()):
    return pl.pallas_call(
        kernel,
        out_shape=out_shape,
        in_specs=in_specs,
        out_specs=vmem(),
        scratch_shapes=list(scratch),
        compiler_params=pltpu.CompilerParams(vmem_limit_bytes=40 * 1024 * 1024),
        cost_estimate=pl.CostEstimate(flops=1000, bytes_accessed=1000, transcendentals=0),
        name=name,
    )


def body(tiles, nbr_tiles, nbr_mask, tile_count, w_query, w_key, w_value, w_out, key_gain):
    own_tiles = tiles[0]
    rows, width = own_tiles.shape
    tile_devices = lax.axis_size("tile")
    fsdp = lax.axis_size("fsdp")
    regions = nbr_tiles.shape[1]
    block = regions // REGIONS_PER_KEY

    shard = w_query.shape[0]
    halves = pl.pallas_call(
        halves_kernel,
        out_shape=jax.ShapeDtypeStruct((2, shard, width // 2), BF16),
        in_specs=[anywhere()] * 2,
        out_specs=vmem(),
        scratch_shapes=[pltpu.SemaphoreType.DMA((2,))],
        name="halves",
    )(w_value, w_out)
    near_halves = from_chips(halves)

    slots = jnp.where(nbr_mask[0] > 0, nbr_tiles[0] + 1, 0)
    mate = swap(slots, "tile", 1)
    inner = [(i, i + 1) for i in range(1, tile_devices - 1, 2)]
    other = lax.ppermute(slots, "tile", inner + [(b, a) for a, b in inner])
    near_query = from_chips(behind(w_query, slots))
    near_key = from_chips(behind(w_key, slots))
    mine = local_call(
        pool_kernel,
        jax.ShapeDtypeStruct((3 * block, width), F32),
        [vmem()] * 4,
        "pool",
    )(slots, mate, other, own_tiles)
    mates = [swap(behind(w, mine), "fsdp", 1) for w in (w_query, w_key, w_value, w_out)]
    pair = local_call(
        pair_kernel,
        jax.ShapeDtypeStruct((6 * block, width), BF16),
        [vmem()] * 2,
        "pair",
    )(mine, behind(swap(mine, "tile", 1), near_halves, *mates))
    near_halves = behind(near_halves, pair)
    other_halves = swap(near_halves, "tile", 1)
    far_halves = swap(near_halves, "fsdp", 1)
    near_query = behind(near_query, pair)
    query = local_call(
        functools.partial(query_kernel, fsdp),
        jax.ShapeDtypeStruct((rows, width), BF16),
        [vmem()] + [anywhere()] * 4,
        "query",
        [pltpu.VMEM((1, width, width), BF16), pltpu.SemaphoreType.DMA((fsdp,))],
    )(own_tiles, w_query, mates[0], near_query, swap(near_query, "fsdp", 1))
    sums = behind(gather_pairs(pair, "tile"), query, near_key)
    other_halves = behind(other_halves, sums)
    attended = local_call(
        functools.partial(attend_kernel, fsdp, block),
        jax.ShapeDtypeStruct((rows, width), BF16),
        [smem()] + [vmem()] * 3 + [anywhere()] * 12,
        "attend",
        [
            pltpu.VMEM((3, width, width), BF16),
            pltpu.VMEM(((tile_devices + 2) * block, width), F32),
            pltpu.SemaphoreType.DMA((5 * fsdp,)),
        ],
    )(
        tile_count,
        sums,
        key_gain[None, :],
        query,
        *(w_key, w_value, w_out),
        *mates[1:],
        *(near_key, near_halves, other_halves),
        *(swap(near_key, "fsdp", 1), far_halves, swap(other_halves, "fsdp", 1)),
    )
    return attended[None]


def solution(mesh):
    placed = (
        P("fsdp", "tile", None),
        P("fsdp", "tile", None),
        P("fsdp", "tile", None),
        P("fsdp"),
        P("fsdp", None),
        P("fsdp", None),
        P("fsdp", None),
        P("fsdp", None),
        P(),
    )
    return jax.shard_map(
        body, mesh=mesh, in_specs=placed, out_specs=P("fsdp", "tile", None), check_vma=False
    )
```

```python
import functools

import jax
import jax.numpy as jnp
from jax import lax
from jax.experimental import pallas as pl
from jax.experimental.pallas import tpu as pltpu
from jax.sharding import PartitionSpec as P

HEADS = 16
NB = 4
REGIONS_PER_KEY = 8
KEY_DILATION = 2
LANE_GROUPS = 2
F32 = jnp.float32
BF16 = jnp.bfloat16


def vmem():
    return pl.BlockSpec(memory_space=pltpu.VMEM)


def smem():
    return pl.BlockSpec(memory_space=pltpu.SMEM)


def anywhere():
    return pl.BlockSpec(memory_space=pl.ANY)


def over(left, right, left_dim, right_dim, precision=None):
    return lax.dot_general(
        left,
        right,
        (((left_dim,), (right_dim,)), ((), ())),
        precision=precision,
        preferred_element_type=F32,
    )


def pool_kernel(here, mate, other, tiles, out):
    count = tiles.shape[0]
    regions = here.shape[0]
    base = lax.axis_index("tile") * count + 1
    row = lax.broadcasted_iota(jnp.int32, (regions, count), 1) + base
    hits, shares = [], []
    for slots in (here, mate, other):
        hit = jnp.zeros((regions, count), F32)
        live = jnp.zeros((regions, 1), F32)
        for s in range(NB):
            slot = slots[:, s : s + 1]
            hit += (slot == row).astype(F32)
            live += (slot > 0).astype(F32)
        hits.append(hit.astype(BF16))
        shares.append(1.0 / (jnp.maximum(live, 1.0) * REGIONS_PER_KEY))
    sums = over(jnp.concatenate(hits, axis=0), tiles[...], 1, 0)
    sums = sums * jnp.concatenate(shares, axis=0)
    out[...] = jnp.sum(sums.reshape(-1, REGIONS_PER_KEY, sums.shape[1]), axis=1)


def pair_kernel(mine, theirs, out):
    block = mine.shape[0] // 3
    first = mine[:block] + theirs[block : 2 * block]
    second = mine[block : 2 * block] + theirs[:block]
    inner = jnp.concatenate([first, second], axis=0)
    high = inner.astype(BF16)
    out[: 2 * block, :] = high
    out[2 * block : 4 * block, :] = (inner - high.astype(F32)).astype(BF16)
    outer = jnp.concatenate([mine[2 * block :], theirs[2 * block :]], axis=0)
    out[4 * block :, :] = outer.astype(BF16)


def collect(copies, sem):
    started = []
    for n, (src, dst) in enumerate(copies):
        copy = pltpu.make_async_copy(src, dst, sem.at[n])
        copy.start()
        started.append(copy)
    return started


def sorted_rows(normed):
    keys = normed.shape[0]
    half = keys // KEY_DILATION
    row = lax.broadcasted_iota(jnp.int32, (keys, keys), 0)
    column = lax.broadcasted_iota(jnp.int32, (keys, keys), 1)
    wanted = KEY_DILATION * (row % half) + row // half
    return over((column == wanted).astype(BF16), normed, 1, 0).astype(BF16)


def spread(rows, group, wide):
    half = rows.shape[0] // KEY_DILATION
    heads = HEADS // LANE_GROUPS
    size = wide // heads
    part = rows[:, group * wide : (group + 1) * wide].astype(F32)
    lane = lax.broadcasted_iota(jnp.int32, (half, wide), 1)
    out = []
    for head in range(heads):
        parity = head % KEY_DILATION
        mine = (lane >= head * size) & (lane < (head + 1) * size)
        out.append(jnp.where(mine, part[parity * half : (parity + 1) * half], 0.0))
    return jnp.concatenate(out, axis=0).astype(BF16)


def first_rows(fsdp, rows):
    me = lax.axis_index("fsdp")
    chips = fsdp // 2
    chip, core = me // 2, me % 2
    owners = [me, 2 * chip + 1 - core]
    for j in range(1, chips):
        source = 2 * lax.rem(chip - j + chips, chips)
        owners += [source + core, source + 1 - core]
    return [pl.multiple_of(owner * rows, rows) for owner in owners]


def place(fsdp, pieces, held):
    rows = pieces[0].shape[0]
    begins = first_rows(fsdp, rows)
    return [(piece, held.at[pl.ds(begin, rows)]) for piece, begin in zip(pieces, begins)]


def query_kernel(fsdp, tiles, *refs):
    pieces = refs[:fsdp]
    out, held, sem = refs[fsdp:]
    for copy in collect(place(fsdp, pieces, held), sem):
        copy.wait()
    out[...] = over(tiles[...], held[...], 1, 0).astype(BF16)


def attend_kernel(fsdp, block, *refs):
    count, sums, gain, query = refs[:4]
    key_pieces, value_pieces = refs[4 : 4 + fsdp], refs[4 + fsdp : 4 + 2 * fsdp]
    out, held, pooled, sem = refs[4 + 2 * fsdp :]
    device = lax.axis_index("tile")
    started = collect(
        place(fsdp, key_pieces, held.at[0]) + place(fsdp, value_pieces, held.at[1]), sem
    )
    pooled[...] = jnp.zeros_like(pooled)
    pairs = sums.shape[0] // (6 * block)
    for s in range(pairs):
        even = device ^ (2 * s)
        odd = even ^ 1
        blocks = [even, odd, even, odd, even - 1 + 2 * (even % 2), odd - 1 + 2 * (odd % 2)]
        for i, index in enumerate(blocks):
            begin = (6 * s + i) * block
            rows = pl.ds(pl.multiple_of((index + 1) * block, block), block)
            pooled[rows, :] += sums[begin : begin + block, :].astype(F32)
    mean = pooled[block : (2 * pairs + 1) * block, :]
    scale = lax.rsqrt(jnp.mean(mean * mean, axis=1, keepdims=True) + 1e-06)
    normed = (mean * scale * gain[...]).astype(BF16)
    ordered = sorted_rows(normed)
    for copy in started:
        copy.wait()
    keys = over(ordered, held[0], 1, 0).astype(BF16)
    values = over(ordered, held[1], 1, 0).astype(BF16)
    half = keys.shape[0] // KEY_DILATION
    heads = HEADS // LANE_GROUPS
    wide = keys.shape[1] // LANE_GROUPS
    rows = query.shape[0]
    size = wide // heads
    row = lax.broadcasted_iota(jnp.int32, (half, 1), 0)
    valid = [
        (KEY_DILATION * row + parity) * (4 * REGIONS_PER_KEY) < count[0]
        for parity in range(KEY_DILATION)
    ]
    hidden = jnp.concatenate(
        [jnp.where(valid[head % KEY_DILATION], 0.0, -jnp.inf) for head in range(heads)], axis=0
    )
    for group in range(LANE_GROUPS):
        lanes = slice(group * wide, (group + 1) * wide)
        score = over(spread(keys, group, wide), query[:, lanes], 1, 1)
        score = (score * (1.0 / size**0.5) + hidden).reshape(heads, half, rows)
        expo = jnp.exp(score - jnp.max(score, axis=1, keepdims=True))
        share = 1.0 / jnp.sum(expo, axis=1, keepdims=True)
        weight = expo.reshape(heads * half, rows).astype(BF16)
        context = over(spread(values, group, wide), weight, 0, 0).reshape(heads, size, rows)
        out[lanes, :] = (context * share).reshape(wide, rows).astype(BF16)


def near_kernel(fsdp, context, piece, mate, out):
    rows = piece.shape[0]
    begins = first_rows(fsdp, rows)
    total = over(context[pl.ds(begins[0], rows), :], piece[...], 0, 0)
    out[...] = total + over(context[pl.ds(begins[1], rows), :], mate[...], 0, 0)


def far_kernel(fsdp, context, total, *refs):
    pieces, out = refs[:-1], refs[-1]
    rows = pieces[0].shape[0]
    begins = first_rows(fsdp, rows)[2:]
    sums = total[...]
    for begin, piece in zip(begins, pieces):
        sums = sums + over(context[pl.ds(begin, rows), :], piece[...], 0, 0)
    out[...] = sums.astype(out.dtype)


def swap(array, axis, offset):
    count = lax.axis_size(axis)
    return lax.ppermute(array, axis, [(i, i ^ offset) for i in range(count)])


def chip_shift(array, axis, step):
    count = lax.axis_size(axis)
    return lax.ppermute(array, axis, [(i, (i + 2 * step) % count) for i in range(count)])


def behind(array, *others):
    return lax.optimization_barrier((array,) + others)[0]


def from_chips(weight):
    return [chip_shift(weight, "fsdp", j) for j in range(1, lax.axis_size("fsdp") // 2)]


def both_cores(near):
    return [piece for mine in near for piece in (mine, swap(mine, "fsdp", 1))]


def behind_each(arrays, *others):
    return [behind(array, *others) for array in arrays]


def gather_pairs(rows, axis):
    pairs = lax.axis_size(axis) // 2
    held = 1
    while held < pairs:
        width = min(4, pairs // held)
        parts = [rows] + [swap(rows, axis, 2 * held * d) for d in range(1, width)]
        rows = jnp.concatenate(parts, axis=0)
        held *= width
    return rows


def local_call(kernel, out_shape, in_specs, name, scratch=()):
    return pl.pallas_call(
        kernel,
        out_shape=out_shape,
        in_specs=in_specs,
        out_specs=vmem(),
        scratch_shapes=list(scratch),
        compiler_params=pltpu.CompilerParams(vmem_limit_bytes=40 * 1024 * 1024),
        cost_estimate=pl.CostEstimate(flops=1000, bytes_accessed=1000, transcendentals=0),
        name=name,
    )


def body(tiles, nbr_tiles, nbr_mask, tile_count, w_query, w_key, w_value, w_out, key_gain):
    own_tiles = tiles[0]
    rows, width = own_tiles.shape
    tile_devices = lax.axis_size("tile")
    fsdp = lax.axis_size("fsdp")
    regions = nbr_tiles.shape[1]
    block = regions // REGIONS_PER_KEY

    near_query = from_chips(w_query)
    near_key = from_chips(w_key)
    slots = jnp.where(nbr_mask[0] > 0, nbr_tiles[0] + 1, 0)
    mate = swap(slots, "tile", 1)
    inner = [(i, i + 1) for i in range(1, tile_devices - 1, 2)]
    other = lax.ppermute(slots, "tile", inner + [(b, a) for a, b in inner])
    mine = local_call(
        pool_kernel,
        jax.ShapeDtypeStruct((3 * block, width), F32),
        [vmem()] * 4,
        "pool",
    )(slots, mate, other, own_tiles)
    mates = [swap(behind(w, mine), "fsdp", 1) for w in (w_query, w_key, w_value, w_out)]
    near_value = from_chips(behind(w_value, slots))
    near_out = from_chips(behind(w_out, mine))
    all_query = both_cores(near_query)
    pair = local_call(
        pair_kernel,
        jax.ShapeDtypeStruct((6 * block, width), BF16),
        [vmem()] * 2,
        "pair",
    )(mine, behind(swap(mine, "tile", 1), *mates, *all_query, *near_key))
    near_key = behind_each(near_key, pair)
    query = local_call(
        functools.partial(query_kernel, fsdp),
        jax.ShapeDtypeStruct((rows, width), BF16),
        [vmem()] + [anywhere()] * fsdp,
        "query",
        [pltpu.VMEM((width, width), BF16), pltpu.SemaphoreType.DMA((fsdp,))],
    )(behind(own_tiles, pair), w_query, mates[0], *all_query)
    sums = behind(gather_pairs(pair, "tile"), query)
    near_value = behind_each(near_value, sums)
    context = local_call(
        functools.partial(attend_kernel, fsdp, block),
        jax.ShapeDtypeStruct((width, rows), BF16),
        [smem()] + [vmem()] * 3 + [anywhere()] * (2 * fsdp),
        "attend",
        [
            pltpu.VMEM((2, width, width), BF16),
            pltpu.VMEM(((tile_devices + 2) * block, width), F32),
            pltpu.SemaphoreType.DMA((2 * fsdp,)),
        ],
    )(
        tile_count,
        sums,
        key_gain[None, :],
        query,
        *(w_key, mates[1], *both_cores(near_key)),
        *(w_value, mates[2], *both_cores(near_value)),
    )
    total = local_call(
        functools.partial(near_kernel, fsdp),
        jax.ShapeDtypeStruct((rows, width), F32),
        [vmem()] * 3,
        "project_near",
    )(context, w_out, mates[3])
    far_out = both_cores(behind_each(near_out, context))
    attended = local_call(
        functools.partial(far_kernel, fsdp),
        jax.ShapeDtypeStruct((rows, width), BF16),
        [vmem()] * fsdp,
        "project_far",
    )(context, total, *far_out)
    return attended[None]


def solution(mesh):
    placed = (
        P("fsdp", "tile", None),
        P("fsdp", "tile", None),
        P("fsdp", "tile", None),
        P("fsdp"),
        P("fsdp", None),
        P("fsdp", None),
        P("fsdp", None),
        P("fsdp", None),
        P(),
    )
    return jax.shard_map(
        body, mesh=mesh, in_specs=placed, out_specs=P("fsdp", "tile", None), check_vma=False
    )
```

```python
import functools

import jax
import jax.numpy as jnp
from jax import lax
from jax.experimental import pallas as pl
from jax.experimental.pallas import tpu as pltpu
from jax.sharding import PartitionSpec as P

HEADS = 16
NB = 4
REGIONS_PER_KEY = 8
KEY_DILATION = 2
LANE_GROUPS = 2
F32 = jnp.float32
BF16 = jnp.bfloat16


def vmem():
    return pl.BlockSpec(memory_space=pltpu.VMEM)


def smem():
    return pl.BlockSpec(memory_space=pltpu.SMEM)


def anywhere():
    return pl.BlockSpec(memory_space=pl.ANY)


def over(left, right, left_dim, right_dim, precision=None):
    return lax.dot_general(
        left,
        right,
        (((left_dim,), (right_dim,)), ((), ())),
        precision=precision,
        preferred_element_type=F32,
    )


def slots_kernel(nbr, mask, out, held, sem):
    count, regions = nbr.shape
    for copy in collect([(nbr, held.at[0]), (mask, held.at[1])], sem):
        copy.wait()
    out[...] = jnp.zeros_like(out)
    out[:count, :regions] = jnp.where(held[1] > 0, held[0] + 1, 0)


def pool_kernel(regions, here, mate, other, tiles, out):
    count = tiles.shape[0]
    base = lax.axis_index("tile") * count + 1
    row = lax.broadcasted_iota(jnp.int32, (regions, count), 1) + base
    hits, shares = [], []
    for slots in (here, mate, other):
        turned = slots[...].T
        hit = jnp.zeros((regions, count), F32)
        live = jnp.zeros((regions, 1), F32)
        for s in range(NB):
            slot = turned[:regions, s : s + 1]
            hit += (slot == row).astype(F32)
            live += (slot > 0).astype(F32)
        hits.append(hit.astype(BF16))
        shares.append(1.0 / (jnp.maximum(live, 1.0) * REGIONS_PER_KEY))
    sums = over(jnp.concatenate(hits, axis=0), tiles[...], 1, 0)
    sums = sums * jnp.concatenate(shares, axis=0)
    out[...] = jnp.sum(sums.reshape(-1, REGIONS_PER_KEY, sums.shape[1]), axis=1)


def pair_kernel(mine, theirs, out):
    block = mine.shape[0] // 3
    first = mine[:block] + theirs[block : 2 * block]
    second = mine[block : 2 * block] + theirs[:block]
    inner = jnp.concatenate([first, second], axis=0)
    high = inner.astype(BF16)
    out[: 2 * block, :] = high
    out[2 * block : 4 * block, :] = (inner - high.astype(F32)).astype(BF16)
    outer = jnp.concatenate([mine[2 * block :], theirs[2 * block :]], axis=0)
    out[4 * block :, :] = outer.astype(BF16)


def collect(copies, sem):
    started = []
    for n, (src, dst) in enumerate(copies):
        copy = pltpu.make_async_copy(src, dst, sem.at[n])
        copy.start()
        started.append(copy)
    return started


def sorted_rows(normed):
    keys = normed.shape[0]
    half = keys // KEY_DILATION
    row = lax.broadcasted_iota(jnp.int32, (keys, keys), 0)
    column = lax.broadcasted_iota(jnp.int32, (keys, keys), 1)
    wanted = KEY_DILATION * (row % half) + row // half
    return over((column == wanted).astype(BF16), normed, 1, 0).astype(BF16)


def spread(rows, group, wide):
    half = rows.shape[0] // KEY_DILATION
    heads = HEADS // LANE_GROUPS
    size = wide // heads
    part = rows[:, group * wide : (group + 1) * wide].astype(F32)
    lane = lax.broadcasted_iota(jnp.int32, (half, wide), 1)
    out = []
    for head in range(heads):
        parity = head % KEY_DILATION
        mine = (lane >= head * size) & (lane < (head + 1) * size)
        out.append(jnp.where(mine, part[parity * half : (parity + 1) * half], 0.0))
    return jnp.concatenate(out, axis=0).astype(BF16)


def place_rows(fsdp, shard, held):
    half_width = held.shape[2] // 2
    chips = fsdp // 2
    me = lax.axis_index("fsdp")
    cut = lax.axis_index("tile") % 2
    chip, core = me // 2, me % 2

    def at(weight, owner, side):
        rows = pl.ds(pl.multiple_of(owner * shard, shard), shard)
        if side is None:
            return held.at[weight, rows]
        columns = pl.ds(pl.multiple_of(side * half_width, half_width), half_width)
        return held.at[weight, rows, columns]

    def own(weight, piece, mate):
        return [(piece, at(weight, me, None)), (mate, at(weight, 2 * chip + 1 - core, None))]

    def others(weight, near, far, side=None):
        copies = []
        for j in range(1, chips):
            source = 2 * lax.rem(chip - j + chips, chips)
            columns = None if side is None else (cut if side == 0 else 1 - cut)
            copies.append((near(j - 1), at(weight, source + core, columns)))
            copies.append((far(j - 1), at(weight, source + 1 - core, columns)))
        return copies

    return own, others


def query_kernel(fsdp, tiles, piece, mate, near, far, out, held, sem):
    own, others = place_rows(fsdp, piece.shape[0], held)
    copies = own(0, piece, mate) + others(0, lambda j: near.at[j], lambda j: far.at[j])
    for copy in collect(copies, sem):
        copy.wait()
    out[...] = over(tiles[...], held[0], 1, 0).astype(BF16)


def attend_kernel(fsdp, block, *refs):
    count, sums, gain, query = refs[:4]
    pieces, mates = refs[4:7], refs[7:10]
    near, far = refs[10:13], refs[13:16]
    out, held, pooled, sem = refs[16:]
    device = lax.axis_index("tile")
    own, others = place_rows(fsdp, pieces[0].shape[0], held)
    copies, ends = [], []
    for weight in (1, 2, 0):
        copies += own(weight, pieces[weight], mates[weight])
        if weight == 0:
            copies += others(0, lambda j: near[0].at[j], lambda j: far[0].at[j])
        else:
            for side in range(2):
                copies += others(
                    weight,
                    lambda j: near[1 + side].at[j, weight - 1],
                    lambda j: far[1 + side].at[j, weight - 1],
                    side,
                )
        ends.append(len(copies))
    started = collect(copies, sem)

    def arrive(begin, end):
        for copy in started[begin:end]:
            copy.wait()

    pooled[...] = jnp.zeros_like(pooled)
    pairs = sums.shape[0] // (6 * block)
    for s in range(pairs):
        even = device ^ (2 * s)
        odd = even ^ 1
        blocks = [even, odd, even, odd, even - 1 + 2 * (even % 2), odd - 1 + 2 * (odd % 2)]
        for i, index in enumerate(blocks):
            begin = (6 * s + i) * block
            rows = pl.ds(pl.multiple_of((index + 1) * block, block), block)
            pooled[rows, :] += sums[begin : begin + block, :].astype(F32)
    mean = pooled[block : (2 * pairs + 1) * block, :]
    scale = lax.rsqrt(jnp.mean(mean * mean, axis=1, keepdims=True) + 1e-06)
    normed = (mean * scale * gain[...]).astype(BF16)
    ordered = sorted_rows(normed)
    arrive(0, ends[0])
    values = over(ordered, held[1], 1, 0).astype(BF16)
    arrive(ends[1], ends[2])
    keys = over(ordered, held[0], 1, 0).astype(BF16)
    half = keys.shape[0] // KEY_DILATION
    heads = HEADS // LANE_GROUPS
    wide = keys.shape[1] // LANE_GROUPS
    rows = query.shape[0]
    size = wide // heads
    row = lax.broadcasted_iota(jnp.int32, (half, 1), 0)
    valid = [
        (KEY_DILATION * row + parity) * (4 * REGIONS_PER_KEY) < count[0]
        for parity in range(KEY_DILATION)
    ]
    hidden = jnp.concatenate(
        [jnp.where(valid[head % KEY_DILATION], 0.0, -jnp.inf) for head in range(heads)], axis=0
    )
    contexts = []
    for group in range(LANE_GROUPS):
        lanes = slice(group * wide, (group + 1) * wide)
        score = over(spread(keys, group, wide), query[:, lanes], 1, 1)
        score = (score * (1.0 / size**0.5) + hidden).reshape(heads, half, rows)
        expo = jnp.exp(score - jnp.max(score, axis=1, keepdims=True))
        share = 1.0 / jnp.sum(expo, axis=1, keepdims=True)
        weight = expo.reshape(heads * half, rows).astype(BF16)
        context = over(spread(values, group, wide), weight, 0, 0).reshape(heads, size, rows)
        contexts.append((context * share).reshape(wide, rows).astype(BF16))
    arrive(ends[0], ends[1])
    context = jnp.concatenate(contexts, axis=0)
    out[...] = over(context, held[2], 0, 0).astype(out.dtype)


def swap(array, axis, offset):
    count = lax.axis_size(axis)
    return lax.ppermute(array, axis, [(i, i ^ offset) for i in range(count)])


def chip_shift(array, axis, step):
    count = lax.axis_size(axis)
    return lax.ppermute(array, axis, [(i, (i + 2 * step) % count) for i in range(count)])


def halves_kernel(w_value, w_out, halves, sem):
    cut = lax.axis_index("tile") % 2
    width = halves.shape[2]
    columns = pl.ds(pl.multiple_of(cut * width, width), width)
    copies = [(w.at[:, columns], halves.at[n]) for n, w in enumerate((w_value, w_out))]
    for copy in collect(copies, sem):
        copy.wait()


def behind(array, *others):
    return lax.optimization_barrier((array,) + others)[0]


def from_chips(weight):
    chips = lax.axis_size("fsdp") // 2
    return jnp.stack([chip_shift(weight, "fsdp", j) for j in range(1, chips)])


def gather_pairs(rows, axis):
    pairs = lax.axis_size(axis) // 2
    held = 1
    while held < pairs:
        width = min(4, pairs // held)
        parts = [rows] + [swap(rows, axis, 2 * held * d) for d in range(1, width)]
        rows = jnp.concatenate(parts, axis=0)
        held *= width
    return rows


def local_call(kernel, out_shape, in_specs, name, scratch=()):
    return pl.pallas_call(
        kernel,
        out_shape=out_shape,
        in_specs=in_specs,
        out_specs=vmem(),
        scratch_shapes=list(scratch),
        compiler_params=pltpu.CompilerParams(vmem_limit_bytes=40 * 1024 * 1024),
        cost_estimate=pl.CostEstimate(flops=1000, bytes_accessed=1000, transcendentals=0),
        name=name,
    )


def body(tiles, nbr_tiles, nbr_mask, tile_count, w_query, w_key, w_value, w_out, key_gain):
    own_tiles = tiles[0]
    rows, width = own_tiles.shape
    tile_devices = lax.axis_size("tile")
    fsdp = lax.axis_size("fsdp")
    regions = nbr_tiles.shape[1]
    block = regions // REGIONS_PER_KEY

    shard = w_query.shape[0]
    near_query = from_chips(w_query)
    slots = local_call(
        slots_kernel,
        jax.ShapeDtypeStruct((8, -(-regions // 128) * 128), jnp.int32),
        [anywhere()] * 2,
        "slots",
        [pltpu.VMEM((2, NB, regions), jnp.int32), pltpu.SemaphoreType.DMA((2,))],
    )(nbr_tiles[0].T, nbr_mask[0].T)
    mate = swap(slots, "tile", 1)
    inner = [(i, i + 1) for i in range(1, tile_devices - 1, 2)]
    other = lax.ppermute(slots, "tile", inner + [(b, a) for a, b in inner])
    halves = local_call(
        halves_kernel,
        jax.ShapeDtypeStruct((2, shard, width // 2), BF16),
        [anywhere()] * 2,
        "halves",
        [pltpu.SemaphoreType.DMA((2,))],
    )(w_value, w_out)
    near_halves = from_chips(halves)
    mine = local_call(
        functools.partial(pool_kernel, regions),
        jax.ShapeDtypeStruct((3 * block, width), F32),
        [vmem()] * 4,
        "pool",
    )(slots, mate, other, behind(own_tiles, near_query))
    near_key = from_chips(behind(w_key, mine))
    mates = [swap(behind(w, mine), "fsdp", 1) for w in (w_query, w_key, w_value, w_out)]
    far_query = swap(near_query, "fsdp", 1)
    pair = local_call(
        pair_kernel,
        jax.ShapeDtypeStruct((6 * block, width), BF16),
        [vmem()] * 2,
        "pair",
    )(mine, behind(swap(mine, "tile", 1), near_halves, far_query, *mates))
    near_halves = behind(near_halves, pair)
    other_halves = swap(near_halves, "tile", 1)
    far_halves = swap(near_halves, "fsdp", 1)
    query = local_call(
        functools.partial(query_kernel, fsdp),
        jax.ShapeDtypeStruct((rows, width), BF16),
        [vmem()] + [anywhere()] * 4,
        "query",
        [pltpu.VMEM((1, width, width), BF16), pltpu.SemaphoreType.DMA((fsdp,))],
    )(behind(own_tiles, pair), w_query, mates[0], near_query, far_query)
    sums = behind(gather_pairs(pair, "tile"), query)
    near_key = behind(near_key, sums)
    other_halves = behind(other_halves, sums)
    attended = local_call(
        functools.partial(attend_kernel, fsdp, block),
        jax.ShapeDtypeStruct((rows, width), BF16),
        [smem()] + [vmem()] * 3 + [anywhere()] * 12,
        "attend",
        [
            pltpu.VMEM((3, width, width), BF16),
            pltpu.VMEM(((tile_devices + 2) * block, width), F32),
            pltpu.SemaphoreType.DMA((5 * fsdp,)),
        ],
    )(
        tile_count,
        sums,
        key_gain[None, :],
        query,
        *(w_key, w_value, w_out),
        *mates[1:],
        *(near_key, near_halves, other_halves),
        *(swap(near_key, "fsdp", 1), far_halves, swap(other_halves, "fsdp", 1)),
    )
    return attended[None]


def solution(mesh):
    placed = (
        P("fsdp", "tile", None),
        P("fsdp", "tile", None),
        P("fsdp", "tile", None),
        P("fsdp"),
        P("fsdp", None),
        P("fsdp", None),
        P("fsdp", None),
        P("fsdp", None),
        P(),
    )
    return jax.shard_map(
        body, mesh=mesh, in_specs=placed, out_specs=P("fsdp", "tile", None), check_vma=False
    )
```

```python
import functools

import jax
import jax.numpy as jnp
from jax import lax
from jax.experimental import pallas as pl
from jax.experimental.pallas import tpu as pltpu
from jax.sharding import PartitionSpec as P

HEADS = 16
NB = 4
REGIONS_PER_KEY = 8
KEY_DILATION = 2
LANE_GROUPS = 2
F32 = jnp.float32
BF16 = jnp.bfloat16


def vmem():
    return pl.BlockSpec(memory_space=pltpu.VMEM)


def smem():
    return pl.BlockSpec(memory_space=pltpu.SMEM)


def anywhere():
    return pl.BlockSpec(memory_space=pl.ANY)


def hbm():
    return pl.BlockSpec(memory_space=pltpu.HBM)


def over(left, right, left_dim, right_dim, precision=None):
    return lax.dot_general(
        left,
        right,
        (((left_dim,), (right_dim,)), ((), ())),
        precision=precision,
        preferred_element_type=F32,
    )


def pool_kernel(regions, here, mate, other, tiles, out):
    count = tiles.shape[0]
    base = lax.axis_index("tile") * count + 1
    row = lax.broadcasted_iota(jnp.int32, (regions, count), 1) + base
    hits, shares = [], []
    for slots in (here, mate, other):
        turned = slots[...].T
        hit = jnp.zeros((regions, count), F32)
        live = jnp.zeros((regions, 1), F32)
        for s in range(NB):
            slot = turned[:regions, s : s + 1]
            hit += (slot == row).astype(F32)
            live += (slot > 0).astype(F32)
        hits.append(hit.astype(BF16))
        shares.append(1.0 / (jnp.maximum(live, 1.0) * REGIONS_PER_KEY))
    sums = over(jnp.concatenate(hits, axis=0), tiles[...], 1, 0)
    sums = sums * jnp.concatenate(shares, axis=0)
    out[...] = jnp.sum(sums.reshape(-1, REGIONS_PER_KEY, sums.shape[1]), axis=1)


def pair_kernel(mine, theirs, out):
    block = mine.shape[0] // 3
    first = mine[:block] + theirs[block : 2 * block]
    second = mine[block : 2 * block] + theirs[:block]
    inner = jnp.concatenate([first, second], axis=0)
    high = inner.astype(BF16)
    out[: 2 * block, :] = high
    out[2 * block : 4 * block, :] = (inner - high.astype(F32)).astype(BF16)
    outer = jnp.concatenate([mine[2 * block :], theirs[2 * block :]], axis=0)
    out[4 * block :, :] = outer.astype(BF16)


def collect(copies, sem):
    started = []
    for n, (src, dst) in enumerate(copies):
        copy = pltpu.make_async_copy(src, dst, sem.at[n])
        copy.start()
        started.append(copy)
    return started


def sorted_rows(normed):
    keys = normed.shape[0]
    half = keys // KEY_DILATION
    row = lax.broadcasted_iota(jnp.int32, (keys, keys), 0)
    column = lax.broadcasted_iota(jnp.int32, (keys, keys), 1)
    wanted = KEY_DILATION * (row % half) + row // half
    return over((column == wanted).astype(BF16), normed, 1, 0).astype(BF16)


def spread(rows, group, wide):
    half = rows.shape[0] // KEY_DILATION
    heads = HEADS // LANE_GROUPS
    size = wide // heads
    part = rows[:, group * wide : (group + 1) * wide].astype(F32)
    lane = lax.broadcasted_iota(jnp.int32, (half, wide), 1)
    out = []
    for head in range(heads):
        parity = head % KEY_DILATION
        mine = (lane >= head * size) & (lane < (head + 1) * size)
        out.append(jnp.where(mine, part[parity * half : (parity + 1) * half], 0.0))
    return jnp.concatenate(out, axis=0).astype(BF16)


def place_rows(fsdp, shard, held):
    half_width = held.shape[2] // 2
    chips = fsdp // 2
    me = lax.axis_index("fsdp")
    cut = lax.axis_index("tile") % 2
    chip, core = me // 2, me % 2

    def at(weight, owner, side):
        rows = pl.ds(pl.multiple_of(owner * shard, shard), shard)
        if side is None:
            return held.at[weight, rows]
        columns = pl.ds(pl.multiple_of(side * half_width, half_width), half_width)
        return held.at[weight, rows, columns]

    def own(weight, piece, mate):
        return [(piece, at(weight, me, None)), (mate, at(weight, 2 * chip + 1 - core, None))]

    def others(weight, near, far, side=None):
        copies = []
        for j in range(1, chips):
            source = 2 * lax.rem(chip - j + chips, chips)
            columns = None if side is None else (cut if side == 0 else 1 - cut)
            copies.append((near(j - 1), at(weight, source + core, columns)))
            copies.append((far(j - 1), at(weight, source + 1 - core, columns)))
        return copies

    return own, others


def query_kernel(fsdp, tiles, piece, mate, near, far, out, held, sem):
    own, others = place_rows(fsdp, piece.shape[0], held)
    copies = own(0, piece, mate) + others(0, lambda j: near.at[j], lambda j: far.at[j])
    for copy in collect(copies, sem):
        copy.wait()
    out[...] = over(tiles[...], held[0], 1, 0).astype(BF16)


def attend_kernel(fsdp, block, *refs):
    count, sums, gain, query = refs[:4]
    pieces, mates = refs[4:7], refs[7:10]
    near, far = refs[10:13], refs[13:16]
    out, held, pooled, sem = refs[16:]
    device = lax.axis_index("tile")
    own, others = place_rows(fsdp, pieces[0].shape[0], held)
    copies, ends = [], []
    for weight in (1, 2, 0):
        copies += own(weight, pieces[weight], mates[weight])
        if weight == 0:
            copies += others(0, lambda j: near[0].at[j], lambda j: far[0].at[j])
        else:
            for side in range(2):
                copies += others(
                    weight,
                    lambda j: near[1 + side].at[j, weight - 1],
                    lambda j: far[1 + side].at[j, weight - 1],
                    side,
                )
        ends.append(len(copies))
    started = collect(copies, sem)

    def arrive(begin, end):
        for copy in started[begin:end]:
            copy.wait()

    pooled[...] = jnp.zeros_like(pooled)
    pairs = sums.shape[0] // (6 * block)
    for s in range(pairs):
        even = device ^ (2 * s)
        odd = even ^ 1
        blocks = [even, odd, even, odd, even - 1 + 2 * (even % 2), odd - 1 + 2 * (odd % 2)]
        for i, index in enumerate(blocks):
            begin = (6 * s + i) * block
            rows = pl.ds(pl.multiple_of((index + 1) * block, block), block)
            pooled[rows, :] += sums[begin : begin + block, :].astype(F32)
    mean = pooled[block : (2 * pairs + 1) * block, :]
    scale = lax.rsqrt(jnp.mean(mean * mean, axis=1, keepdims=True) + 1e-06)
    normed = (mean * scale * gain[...]).astype(BF16)
    ordered = sorted_rows(normed)
    arrive(0, ends[0])
    values = over(ordered, held[1], 1, 0).astype(BF16)
    arrive(ends[1], ends[2])
    keys = over(ordered, held[0], 1, 0).astype(BF16)
    half = keys.shape[0] // KEY_DILATION
    heads = HEADS // LANE_GROUPS
    wide = keys.shape[1] // LANE_GROUPS
    rows = query.shape[0]
    size = wide // heads
    row = lax.broadcasted_iota(jnp.int32, (half, 1), 0)
    valid = [
        (KEY_DILATION * row + parity) * (4 * REGIONS_PER_KEY) < count[0]
        for parity in range(KEY_DILATION)
    ]
    hidden = jnp.concatenate(
        [jnp.where(valid[head % KEY_DILATION], 0.0, -jnp.inf) for head in range(heads)], axis=0
    )
    contexts = []
    for group in range(LANE_GROUPS):
        lanes = slice(group * wide, (group + 1) * wide)
        score = over(spread(keys, group, wide), query[:, lanes], 1, 1)
        score = (score * (1.0 / size**0.5) + hidden).reshape(heads, half, rows)
        expo = jnp.exp(score - jnp.max(score, axis=1, keepdims=True))
        share = 1.0 / jnp.sum(expo, axis=1, keepdims=True)
        weight = expo.reshape(heads * half, rows).astype(BF16)
        context = over(spread(values, group, wide), weight, 0, 0).reshape(heads, size, rows)
        contexts.append((context * share).reshape(wide, rows).astype(BF16))
    arrive(ends[0], ends[1])
    context = jnp.concatenate(contexts, axis=0)
    out[...] = over(context, held[2], 0, 0).astype(out.dtype)


def swap(array, axis, offset):
    count = lax.axis_size(axis)
    return lax.ppermute(array, axis, [(i, i ^ offset) for i in range(count)])


def chip_shift(array, axis, step):
    count = lax.axis_size(axis)
    return lax.ppermute(array, axis, [(i, (i + 2 * step) % count) for i in range(count)])


def halves_kernel(w_value, w_out, halves, sem):
    cut = lax.axis_index("tile") % 2
    width = halves.shape[2]
    columns = pl.ds(pl.multiple_of(cut * width, width), width)
    copies = [(w.at[:, columns], halves.at[n]) for n, w in enumerate((w_value, w_out))]
    for copy in collect(copies, sem):
        copy.wait()


def behind(array, *others):
    return lax.optimization_barrier((array,) + others)[0]


def from_chips(weight):
    chips = lax.axis_size("fsdp") // 2
    return jnp.stack([chip_shift(weight, "fsdp", j) for j in range(1, chips)])


def gather_pairs(rows, axis):
    pairs = lax.axis_size(axis) // 2
    held = 1
    while held < pairs:
        width = min(4, pairs // held)
        parts = [rows] + [swap(rows, axis, 2 * held * d) for d in range(1, width)]
        rows = jnp.concatenate(parts, axis=0)
        held *= width
    return rows


def local_call(kernel, out_shape, in_specs, name, scratch=()):
    return pl.pallas_call(
        kernel,
        out_shape=out_shape,
        in_specs=in_specs,
        out_specs=vmem(),
        scratch_shapes=list(scratch),
        compiler_params=pltpu.CompilerParams(vmem_limit_bytes=40 * 1024 * 1024),
        cost_estimate=pl.CostEstimate(flops=1000, bytes_accessed=1000, transcendentals=0),
        name=name,
    )


def body(tiles, nbr_tiles, nbr_mask, tile_count, w_query, w_key, w_value, w_out, key_gain):
    own_tiles = tiles[0]
    rows, width = own_tiles.shape
    tile_devices = lax.axis_size("tile")
    fsdp = lax.axis_size("fsdp")
    regions = nbr_tiles.shape[1]
    block = regions // REGIONS_PER_KEY

    shard = w_query.shape[0]
    near_query = from_chips(w_query)
    slots = jnp.where(nbr_mask[0].T > 0, nbr_tiles[0].T + 1, 0)
    slots = jnp.pad(slots, ((0, 8 - NB), (0, -regions % 128)))
    mate = swap(slots, "tile", 1)
    inner = [(i, (i + 1) % tile_devices) for i in range(1, tile_devices, 2)]
    other = lax.ppermute(slots, "tile", inner + [(b, a) for a, b in inner])
    halves = pl.pallas_call(
        halves_kernel,
        out_shape=jax.ShapeDtypeStruct((2, shard, width // 2), BF16),
        in_specs=[hbm()] * 2,
        out_specs=vmem(),
        scratch_shapes=[pltpu.SemaphoreType.DMA((2,))],
        name="halves",
    )(behind(w_value, slots), w_out)
    near_halves = from_chips(behind(halves, mate, other))
    mine = local_call(
        functools.partial(pool_kernel, regions),
        jax.ShapeDtypeStruct((3 * block, width), F32),
        [vmem()] * 4,
        "pool",
    )(slots, mate, other, behind(own_tiles, near_query))
    near_key = from_chips(behind(w_key, mine))
    mates = [swap(behind(w, mine), "fsdp", 1) for w in (w_query, w_key, w_value, w_out)]
    far_query = swap(near_query, "fsdp", 1)
    pair = local_call(
        pair_kernel,
        jax.ShapeDtypeStruct((6 * block, width), BF16),
        [vmem()] * 2,
        "pair",
    )(mine, behind(swap(mine, "tile", 1), near_halves, far_query, *mates))
    near_halves = behind(near_halves, pair)
    other_halves = swap(near_halves, "tile", 1)
    far_halves = swap(near_halves, "fsdp", 1)
    query = local_call(
        functools.partial(query_kernel, fsdp),
        jax.ShapeDtypeStruct((rows, width), BF16),
        [vmem()] + [anywhere()] * 4,
        "query",
        [pltpu.VMEM((1, width, width), BF16), pltpu.SemaphoreType.DMA((fsdp,))],
    )(behind(own_tiles, pair), w_query, mates[0], near_query, far_query)
    sums = behind(gather_pairs(pair, "tile"), query)
    near_key = behind(near_key, sums)
    other_halves = behind(other_halves, sums)
    attended = local_call(
        functools.partial(attend_kernel, fsdp, block),
        jax.ShapeDtypeStruct((rows, width), BF16),
        [smem()] + [vmem()] * 3 + [anywhere()] * 12,
        "attend",
        [
            pltpu.VMEM((3, width, width), BF16),
            pltpu.VMEM(((tile_devices + 2) * block, width), F32),
            pltpu.SemaphoreType.DMA((5 * fsdp,)),
        ],
    )(
        tile_count,
        sums,
        key_gain[None, :],
        query,
        *(w_key, w_value, w_out),
        *mates[1:],
        *(near_key, near_halves, other_halves),
        *(swap(near_key, "fsdp", 1), far_halves, swap(other_halves, "fsdp", 1)),
    )
    return attended[None]


def solution(mesh):
    placed = (
        P("fsdp", "tile", None),
        P("fsdp", "tile", None),
        P("fsdp", "tile", None),
        P("fsdp"),
        P("fsdp", None),
        P("fsdp", None),
        P("fsdp", None),
        P("fsdp", None),
        P(),
    )
    return jax.shard_map(
        body, mesh=mesh, in_specs=placed, out_specs=P("fsdp", "tile", None), check_vma=False
    )
```

```python
import functools

import jax
import jax.numpy as jnp
from jax import lax
from jax.experimental import pallas as pl
from jax.experimental.pallas import tpu as pltpu
from jax.sharding import PartitionSpec as P

HEADS = 16
NB = 4
REGIONS_PER_KEY = 8
KEY_DILATION = 2
LANE_GROUPS = 2
F32 = jnp.float32
BF16 = jnp.bfloat16


def vmem():
    return pl.BlockSpec(memory_space=pltpu.VMEM)


def smem():
    return pl.BlockSpec(memory_space=pltpu.SMEM)


def anywhere():
    return pl.BlockSpec(memory_space=pl.ANY)


def hbm():
    return pl.BlockSpec(memory_space=pltpu.HBM)


def over(left, right, left_dim, right_dim, precision=None):
    return lax.dot_general(
        left,
        right,
        (((left_dim,), (right_dim,)), ((), ())),
        precision=precision,
        preferred_element_type=F32,
    )


def pool_kernel(regions, here, mate, other, tiles, out):
    count = tiles.shape[0]
    base = lax.axis_index("tile") * count + 1
    row = lax.broadcasted_iota(jnp.int32, (regions, count), 1) + base
    hits, shares = [], []
    for slots in (here, mate, other):
        turned = slots[...].T
        hit = jnp.zeros((regions, count), F32)
        live = jnp.zeros((regions, 1), F32)
        for s in range(NB):
            slot = turned[:regions, s : s + 1]
            hit += (slot == row).astype(F32)
            live += (slot > 0).astype(F32)
        hits.append(hit.astype(BF16))
        shares.append(1.0 / (jnp.maximum(live, 1.0) * REGIONS_PER_KEY))
    sums = over(jnp.concatenate(hits, axis=0), tiles[...], 1, 0)
    sums = sums * jnp.concatenate(shares, axis=0)
    out[...] = jnp.sum(sums.reshape(-1, REGIONS_PER_KEY, sums.shape[1]), axis=1)


def pair_kernel(mine, theirs, out):
    block = mine.shape[0] // 3
    first = mine[:block] + theirs[block : 2 * block]
    second = mine[block : 2 * block] + theirs[:block]
    inner = jnp.concatenate([first, second], axis=0)
    high = inner.astype(BF16)
    out[: 2 * block, :] = high
    out[2 * block : 4 * block, :] = (inner - high.astype(F32)).astype(BF16)
    outer = jnp.concatenate([mine[2 * block :], theirs[2 * block :]], axis=0)
    out[4 * block :, :] = outer.astype(BF16)


def collect(copies, sem):
    started = []
    for n, (src, dst) in enumerate(copies):
        copy = pltpu.make_async_copy(src, dst, sem.at[n])
        copy.start()
        started.append(copy)
    return started


def sorted_rows(normed):
    keys = normed.shape[0]
    half = keys // KEY_DILATION
    row = lax.broadcasted_iota(jnp.int32, (keys, keys), 0)
    column = lax.broadcasted_iota(jnp.int32, (keys, keys), 1)
    wanted = KEY_DILATION * (row % half) + row // half
    return over((column == wanted).astype(BF16), normed, 1, 0).astype(BF16)


def spread(rows, group, wide):
    half = rows.shape[0] // KEY_DILATION
    heads = HEADS // LANE_GROUPS
    size = wide // heads
    part = rows[:, group * wide : (group + 1) * wide].astype(F32)
    lane = lax.broadcasted_iota(jnp.int32, (half, wide), 1)
    out = []
    for head in range(heads):
        parity = head % KEY_DILATION
        mine = (lane >= head * size) & (lane < (head + 1) * size)
        out.append(jnp.where(mine, part[parity * half : (parity + 1) * half], 0.0))
    return jnp.concatenate(out, axis=0).astype(BF16)


def place_rows(fsdp, shard, held):
    half_width = held.shape[2] // 2
    chips = fsdp // 2
    me = lax.axis_index("fsdp")
    cut = lax.axis_index("tile") % 2
    chip, core = me // 2, me % 2

    def at(weight, owner, side):
        rows = pl.ds(pl.multiple_of(owner * shard, shard), shard)
        if side is None:
            return held.at[weight, rows]
        columns = pl.ds(pl.multiple_of(side * half_width, half_width), half_width)
        return held.at[weight, rows, columns]

    def own(weight, piece, mate):
        return [(piece, at(weight, me, None)), (mate, at(weight, 2 * chip + 1 - core, None))]

    def others(weight, near, far, side=None):
        copies = []
        for j in range(1, chips):
            source = 2 * lax.rem(chip - j + chips, chips)
            columns = None if side is None else (cut if side == 0 else 1 - cut)
            copies.append((near(j - 1), at(weight, source + core, columns)))
            copies.append((far(j - 1), at(weight, source + 1 - core, columns)))
        return copies

    return own, others


def attend_kernel(fsdp, block, *refs):
    count, sums, gain, tiles = refs[:4]
    pieces, mates = refs[4:8], refs[8:12]
    near, far = refs[12:16], refs[16:20]
    out, held, pooled, sem = refs[20:]
    device = lax.axis_index("tile")
    own, others = place_rows(fsdp, pieces[0].shape[0], held)
    copies, ends = [], []
    for weight in range(4):
        copies += own(weight, pieces[weight], mates[weight])
        if weight < 2:
            copies += others(weight, lambda j: near[weight].at[j], lambda j: far[weight].at[j])
        else:
            for side in range(2):
                copies += others(
                    weight,
                    lambda j: near[2 + side].at[j, weight - 2],
                    lambda j: far[2 + side].at[j, weight - 2],
                    side,
                )
        ends.append(len(copies))
    started = collect(copies, sem)

    def arrive(weight):
        for copy in started[(ends[weight - 1] if weight else 0) : ends[weight]]:
            copy.wait()

    arrive(0)
    query = over(tiles[...], held[0], 1, 0).astype(BF16)
    pooled[...] = jnp.zeros_like(pooled)
    pairs = sums.shape[0] // (6 * block)
    for s in range(pairs):
        even = device ^ (2 * s)
        odd = even ^ 1
        blocks = [even, odd, even, odd, even - 1 + 2 * (even % 2), odd - 1 + 2 * (odd % 2)]
        for i, index in enumerate(blocks):
            begin = (6 * s + i) * block
            rows = pl.ds(pl.multiple_of((index + 1) * block, block), block)
            pooled[rows, :] += sums[begin : begin + block, :].astype(F32)
    mean = pooled[block : (2 * pairs + 1) * block, :]
    scale = lax.rsqrt(jnp.mean(mean * mean, axis=1, keepdims=True) + 1e-06)
    normed = (mean * scale * gain[...]).astype(BF16)
    ordered = sorted_rows(normed)
    arrive(1)
    keys = over(ordered, held[1], 1, 0).astype(BF16)
    arrive(2)
    values = over(ordered, held[2], 1, 0).astype(BF16)
    half = keys.shape[0] // KEY_DILATION
    heads = HEADS // LANE_GROUPS
    wide = keys.shape[1] // LANE_GROUPS
    rows = query.shape[0]
    size = wide // heads
    row = lax.broadcasted_iota(jnp.int32, (half, 1), 0)
    valid = [
        (KEY_DILATION * row + parity) * (4 * REGIONS_PER_KEY) < count[0]
        for parity in range(KEY_DILATION)
    ]
    hidden = jnp.concatenate(
        [jnp.where(valid[head % KEY_DILATION], 0.0, -jnp.inf) for head in range(heads)], axis=0
    )
    contexts = []
    for group in range(LANE_GROUPS):
        lanes = slice(group * wide, (group + 1) * wide)
        score = over(spread(keys, group, wide), query[:, lanes], 1, 1)
        score = (score * (1.0 / size**0.5) + hidden).reshape(heads, half, rows)
        expo = jnp.exp(score - jnp.max(score, axis=1, keepdims=True))
        share = 1.0 / jnp.sum(expo, axis=1, keepdims=True)
        weight = expo.reshape(heads * half, rows).astype(BF16)
        context = over(spread(values, group, wide), weight, 0, 0).reshape(heads, size, rows)
        contexts.append((context * share).reshape(wide, rows).astype(BF16))
    arrive(3)
    context = jnp.concatenate(contexts, axis=0)
    out[...] = over(context, held[3], 0, 0).astype(out.dtype)


def swap(array, axis, offset):
    count = lax.axis_size(axis)
    return lax.ppermute(array, axis, [(i, i ^ offset) for i in range(count)])


def chip_shift(array, axis, step):
    count = lax.axis_size(axis)
    return lax.ppermute(array, axis, [(i, (i + 2 * step) % count) for i in range(count)])


def halves_kernel(w_value, w_out, halves, sem):
    cut = lax.axis_index("tile") % 2
    width = halves.shape[2]
    columns = pl.ds(pl.multiple_of(cut * width, width), width)
    copies = [(w.at[:, columns], halves.at[n]) for n, w in enumerate((w_value, w_out))]
    for copy in collect(copies, sem):
        copy.wait()


def behind(array, *others):
    return lax.optimization_barrier((array,) + others)[0]


def from_chips(weight):
    chips = lax.axis_size("fsdp") // 2
    return jnp.stack([chip_shift(weight, "fsdp", j) for j in range(1, chips)])


def gather_pairs(rows, axis):
    pairs = lax.axis_size(axis) // 2
    held = 1
    while held < pairs:
        width = min(4, pairs // held)
        parts = [rows] + [swap(rows, axis, 2 * held * d) for d in range(1, width)]
        rows = jnp.concatenate(parts, axis=0)
        held *= width
    return rows


def local_call(kernel, out_shape, in_specs, name, scratch=()):
    return pl.pallas_call(
        kernel,
        out_shape=out_shape,
        in_specs=in_specs,
        out_specs=vmem(),
        scratch_shapes=list(scratch),
        compiler_params=pltpu.CompilerParams(vmem_limit_bytes=40 * 1024 * 1024),
        cost_estimate=pl.CostEstimate(flops=1000, bytes_accessed=1000, transcendentals=0),
        name=name,
    )


def body(tiles, nbr_tiles, nbr_mask, tile_count, w_query, w_key, w_value, w_out, key_gain):
    own_tiles = tiles[0]
    rows, width = own_tiles.shape
    tile_devices = lax.axis_size("tile")
    fsdp = lax.axis_size("fsdp")
    regions = nbr_tiles.shape[1]
    block = regions // REGIONS_PER_KEY

    shard = w_query.shape[0]
    near_query = from_chips(w_query)
    slots = jnp.where(nbr_mask[0].T > 0, nbr_tiles[0].T + 1, 0)
    slots = jnp.pad(slots, ((0, 8 - NB), (0, -regions % 128)))
    mate = swap(slots, "tile", 1)
    inner = [(i, i + 1) for i in range(1, tile_devices - 1, 2)]
    ends = [(0, 0), (tile_devices - 1, tile_devices - 1)]
    other = lax.ppermute(slots, "tile", inner + [(b, a) for a, b in inner] + ends)
    halves = pl.pallas_call(
        halves_kernel,
        out_shape=jax.ShapeDtypeStruct((2, shard, width // 2), BF16),
        in_specs=[hbm()] * 2,
        out_specs=vmem(),
        scratch_shapes=[pltpu.SemaphoreType.DMA((2,))],
        name="halves",
    )(behind(w_value, slots), w_out)
    near_halves = from_chips(behind(halves, mate, other))
    mine = local_call(
        functools.partial(pool_kernel, regions),
        jax.ShapeDtypeStruct((3 * block, width), F32),
        [vmem()] * 4,
        "pool",
    )(slots, mate, other, behind(own_tiles, halves))
    near_key = from_chips(behind(w_key, mine))
    pair = local_call(
        pair_kernel,
        jax.ShapeDtypeStruct((6 * block, width), BF16),
        [vmem()] * 2,
        "pair",
    )(mine, behind(swap(mine, "tile", 1), near_query))
    near_halves = behind(near_halves, pair)
    other_halves = swap(near_halves, "tile", 1)
    far_halves = swap(near_halves, "fsdp", 1)
    sums = gather_pairs(pair, "tile")
    near_query = behind(near_query, sums)
    weights = (w_query, w_key, w_value, w_out)
    mates = [swap(behind(w, sums), "fsdp", 1) for w in weights]
    far_query = swap(near_query, "fsdp", 1)
    near_key = behind(near_key, sums)
    near = (near_query, near_key, near_halves, other_halves)
    far = (far_query, swap(near_key, "fsdp", 1), far_halves, swap(behind(other_halves, sums), "fsdp", 1))
    attended = local_call(
        functools.partial(attend_kernel, fsdp, block),
        jax.ShapeDtypeStruct((rows, width), BF16),
        [smem()] + [vmem()] * 3 + [anywhere()] * 16,
        "attend",
        [
            pltpu.VMEM((4, width, width), BF16),
            pltpu.VMEM(((tile_devices + 2) * block, width), F32),
            pltpu.SemaphoreType.DMA((6 * fsdp,)),
        ],
    )(tile_count, sums, key_gain[None, :], own_tiles, *weights, *mates, *near, *far)
    return attended[None]


def solution(mesh):
    placed = (
        P("fsdp", "tile", None),
        P("fsdp", "tile", None),
        P("fsdp", "tile", None),
        P("fsdp"),
        P("fsdp", None),
        P("fsdp", None),
        P("fsdp", None),
        P("fsdp", None),
        P(),
    )
    return jax.shard_map(
        body, mesh=mesh, in_specs=placed, out_specs=P("fsdp", "tile", None), check_vma=False
    )
```

```python
import functools

import jax
import jax.numpy as jnp
from jax import lax
from jax.experimental import pallas as pl
from jax.experimental.pallas import tpu as pltpu
from jax.sharding import PartitionSpec as P

HEADS = 16
NB = 4
REGIONS_PER_KEY = 8
KEY_DILATION = 2
LANE_GROUPS = 2
F32 = jnp.float32
BF16 = jnp.bfloat16


def vmem():
    return pl.BlockSpec(memory_space=pltpu.VMEM)


def smem():
    return pl.BlockSpec(memory_space=pltpu.SMEM)


def anywhere():
    return pl.BlockSpec(memory_space=pl.ANY)


def hbm():
    return pl.BlockSpec(memory_space=pltpu.HBM)


def over(left, right, left_dim, right_dim, precision=None):
    return lax.dot_general(
        left,
        right,
        (((left_dim,), (right_dim,)), ((), ())),
        precision=precision,
        preferred_element_type=F32,
    )


def pool_kernel(regions, here, mate, other, tiles, out):
    count = tiles.shape[0]
    base = lax.axis_index("tile") * count + 1
    row = lax.broadcasted_iota(jnp.int32, (regions, count), 1) + base
    hits, shares = [], []
    for slots in (here, mate, other):
        turned = slots[...].T
        hit = jnp.zeros((regions, count), F32)
        live = jnp.zeros((regions, 1), F32)
        for s in range(NB):
            slot = turned[:regions, s : s + 1]
            hit += (slot == row).astype(F32)
            live += (slot > 0).astype(F32)
        hits.append(hit.astype(BF16))
        shares.append(1.0 / (jnp.maximum(live, 1.0) * REGIONS_PER_KEY))
    sums = over(jnp.concatenate(hits, axis=0), tiles[...], 1, 0)
    sums = sums * jnp.concatenate(shares, axis=0)
    out[...] = jnp.sum(sums.reshape(-1, REGIONS_PER_KEY, sums.shape[1]), axis=1)


def pair_kernel(mine, theirs, out):
    block = mine.shape[0] // 3
    first = mine[:block] + theirs[block : 2 * block]
    second = mine[block : 2 * block] + theirs[:block]
    inner = jnp.concatenate([first, second], axis=0)
    high = inner.astype(BF16)
    out[: 2 * block, :] = high
    out[2 * block : 4 * block, :] = (inner - high.astype(F32)).astype(BF16)
    outer = jnp.concatenate([mine[2 * block :], theirs[2 * block :]], axis=0)
    out[4 * block :, :] = outer.astype(BF16)


def collect(copies, sem):
    started = []
    for n, (src, dst) in enumerate(copies):
        copy = pltpu.make_async_copy(src, dst, sem.at[n])
        copy.start()
        started.append(copy)
    return started


def sorted_rows(normed):
    keys = normed.shape[0]
    half = keys // KEY_DILATION
    row = lax.broadcasted_iota(jnp.int32, (keys, keys), 0)
    column = lax.broadcasted_iota(jnp.int32, (keys, keys), 1)
    wanted = KEY_DILATION * (row % half) + row // half
    return over((column == wanted).astype(BF16), normed, 1, 0).astype(BF16)


def spread(rows, group, wide):
    half = rows.shape[0] // KEY_DILATION
    heads = HEADS // LANE_GROUPS
    size = wide // heads
    part = rows[:, group * wide : (group + 1) * wide].astype(F32)
    lane = lax.broadcasted_iota(jnp.int32, (half, wide), 1)
    out = []
    for head in range(heads):
        parity = head % KEY_DILATION
        mine = (lane >= head * size) & (lane < (head + 1) * size)
        out.append(jnp.where(mine, part[parity * half : (parity + 1) * half], 0.0))
    return jnp.concatenate(out, axis=0).astype(BF16)


def place_rows(fsdp, shard, held):
    half_width = held.shape[2] // 2
    chips = fsdp // 2
    me = lax.axis_index("fsdp")
    chip, core = me // 2, me % 2

    def at(weight, owner, side):
        rows = pl.ds(pl.multiple_of(owner * shard, shard), shard)
        if side is None:
            return held.at[weight, rows]
        columns = pl.ds(pl.multiple_of(side * half_width, half_width), half_width)
        return held.at[weight, rows, columns]

    def own(weight, piece, mate):
        return [(piece, at(weight, me, None)), (mate, at(weight, 2 * chip + 1 - core, None))]

    def others(weight, near, far, columns=None):
        copies = []
        for j in range(1, chips):
            source = 2 * lax.rem(chip - j + chips, chips)
            copies.append((near(j - 1), at(weight, source + core, columns)))
            copies.append((far(j - 1), at(weight, source + 1 - core, columns)))
        return copies

    return own, others


def attend_kernel(fsdp, block, *refs):
    count, sums, gain, tiles = refs[:4]
    pieces, mates = refs[4:8], refs[8:12]
    near, far = refs[12:15], refs[15:18]
    out, held, pooled, sem = refs[18:]
    device = lax.axis_index("tile")
    cut = device % 2
    own, others = place_rows(fsdp, pieces[0].shape[0], held)

    def from_others(weight, piece, part, columns):
        return others(
            weight, lambda j: near[piece].at[j, part], lambda j: far[piece].at[j, part], columns
        )

    copies, ends = [], []
    for weight in range(4):
        copies += own(weight, pieces[weight], mates[weight])
        if weight == 0:
            copies += from_others(0, 0, 0, 0) + from_others(0, 0, 1, 1)
        elif weight == 1:
            copies += others(1, lambda j: near[1].at[j], lambda j: far[1].at[j])
        else:
            copies += from_others(weight, 0, weight, cut)
            copies += from_others(weight, 2, weight - 2, 1 - cut)
        ends.append(len(copies))
    started = collect(copies, sem)

    def arrive(weight):
        for copy in started[(ends[weight - 1] if weight else 0) : ends[weight]]:
            copy.wait()

    arrive(0)
    query = over(tiles[...], held[0], 1, 0).astype(BF16)
    pooled[...] = jnp.zeros_like(pooled)
    pairs = sums.shape[0] // (6 * block)
    for s in range(pairs):
        even = device ^ (2 * s)
        odd = even ^ 1
        blocks = [even, odd, even, odd, even - 1 + 2 * (even % 2), odd - 1 + 2 * (odd % 2)]
        for i, index in enumerate(blocks):
            begin = (6 * s + i) * block
            rows = pl.ds(pl.multiple_of((index + 1) * block, block), block)
            pooled[rows, :] += sums[begin : begin + block, :].astype(F32)
    mean = pooled[block : (2 * pairs + 1) * block, :]
    scale = lax.rsqrt(jnp.mean(mean * mean, axis=1, keepdims=True) + 1e-06)
    normed = (mean * scale * gain[...]).astype(BF16)
    ordered = sorted_rows(normed)
    arrive(1)
    keys = over(ordered, held[1], 1, 0).astype(BF16)
    arrive(2)
    values = over(ordered, held[2], 1, 0).astype(BF16)
    half = keys.shape[0] // KEY_DILATION
    heads = HEADS // LANE_GROUPS
    wide = keys.shape[1] // LANE_GROUPS
    rows = query.shape[0]
    size = wide // heads
    row = lax.broadcasted_iota(jnp.int32, (half, 1), 0)
    valid = [
        (KEY_DILATION * row + parity) * (4 * REGIONS_PER_KEY) < count[0]
        for parity in range(KEY_DILATION)
    ]
    hidden = jnp.concatenate(
        [jnp.where(valid[head % KEY_DILATION], 0.0, -jnp.inf) for head in range(heads)], axis=0
    )
    contexts = []
    for group in range(LANE_GROUPS):
        lanes = slice(group * wide, (group + 1) * wide)
        score = over(spread(keys, group, wide), query[:, lanes], 1, 1)
        score = (score * (1.0 / size**0.5) + hidden).reshape(heads, half, rows)
        expo = jnp.exp(score - jnp.max(score, axis=1, keepdims=True))
        share = 1.0 / jnp.sum(expo, axis=1, keepdims=True)
        weight = expo.reshape(heads * half, rows).astype(BF16)
        context = over(spread(values, group, wide), weight, 0, 0).reshape(heads, size, rows)
        contexts.append((context * share).reshape(wide, rows).astype(BF16))
    arrive(3)
    context = jnp.concatenate(contexts, axis=0)
    out[...] = over(context, held[3], 0, 0).astype(out.dtype)


def swap(array, axis, offset):
    count = lax.axis_size(axis)
    return lax.ppermute(array, axis, [(i, i ^ offset) for i in range(count)])


def chip_shift(array, axis, step):
    count = lax.axis_size(axis)
    return lax.ppermute(array, axis, [(i, (i + 2 * step) % count) for i in range(count)])


def stack_kernel(w_query, w_value, w_out, stack, sem):
    cut = lax.axis_index("tile") % 2
    width = stack.shape[2]
    halves = ((w_query, 0), (w_query, 1), (w_value, cut), (w_out, cut))
    copies = []
    for n, (w, half) in enumerate(halves):
        columns = pl.ds(pl.multiple_of(half * width, width), width)
        copies.append((w.at[:, columns], stack.at[n]))
    for copy in collect(copies, sem):
        copy.wait()


def behind(array, *others):
    return lax.optimization_barrier((array,) + others)[0]


def from_chips(weight):
    chips = lax.axis_size("fsdp") // 2
    return jnp.stack([chip_shift(weight, "fsdp", j) for j in range(1, chips)])


def gather_pairs(rows, axis):
    pairs = lax.axis_size(axis) // 2
    held = 1
    while held < pairs:
        width = min(4, pairs // held)
        parts = [rows] + [swap(rows, axis, 2 * held * d) for d in range(1, width)]
        rows = jnp.concatenate(parts, axis=0)
        held *= width
    return rows


def local_call(kernel, out_shape, in_specs, name, scratch=()):
    return pl.pallas_call(
        kernel,
        out_shape=out_shape,
        in_specs=in_specs,
        out_specs=vmem(),
        scratch_shapes=list(scratch),
        compiler_params=pltpu.CompilerParams(vmem_limit_bytes=40 * 1024 * 1024),
        cost_estimate=pl.CostEstimate(flops=1000, bytes_accessed=1000, transcendentals=0),
        name=name,
    )


def body(tiles, nbr_tiles, nbr_mask, tile_count, w_query, w_key, w_value, w_out, key_gain):
    own_tiles = tiles[0]
    rows, width = own_tiles.shape
    tile_devices = lax.axis_size("tile")
    fsdp = lax.axis_size("fsdp")
    regions = nbr_tiles.shape[1]
    block = regions // REGIONS_PER_KEY

    shard = w_query.shape[0]
    stack = pl.pallas_call(
        stack_kernel,
        out_shape=jax.ShapeDtypeStruct((4, shard, width // 2), BF16),
        in_specs=[hbm()] * 3,
        out_specs=vmem(),
        scratch_shapes=[pltpu.SemaphoreType.DMA((4,))],
        name="stack",
    )(w_query, w_value, w_out)
    near_stack = from_chips(stack)
    near_key = from_chips(w_key)
    slots = jnp.where(nbr_mask[0].T > 0, nbr_tiles[0].T + 1, 0)
    slots = jnp.pad(slots, ((0, 8 - NB), (0, -regions % 128)))
    mate = swap(slots, "tile", 1)
    inner = [(i, i + 1) for i in range(1, tile_devices - 1, 2)]
    other = lax.ppermute(slots, "tile", inner + [(b, a) for a, b in inner])
    mates = [swap(behind(w, slots), "fsdp", 1) for w in (w_query, w_key)]
    mine = local_call(
        functools.partial(pool_kernel, regions),
        jax.ShapeDtypeStruct((3 * block, width), F32),
        [vmem()] * 4,
        "pool",
    )(slots, mate, other, behind(own_tiles, *mates))
    pair = local_call(
        pair_kernel,
        jax.ShapeDtypeStruct((6 * block, width), BF16),
        [vmem()] * 2,
        "pair",
    )(mine, swap(mine, "tile", 1))
    near_stack = behind(near_stack, pair)
    other_halves = swap(near_stack[:, 2:], "tile", 1)
    sums = gather_pairs(pair, "tile")
    far_stack = swap(behind(near_stack, sums), "fsdp", 1)
    mates += [swap(behind(w, sums), "fsdp", 1) for w in (w_value, w_out)]
    near_key = behind(near_key, sums)
    other_halves = behind(other_halves, sums)
    weights = (w_query, w_key, w_value, w_out)
    near = (near_stack, near_key, other_halves)
    far = (far_stack, swap(near_key, "fsdp", 1), swap(other_halves, "fsdp", 1))
    attended = local_call(
        functools.partial(attend_kernel, fsdp, block),
        jax.ShapeDtypeStruct((rows, width), BF16),
        [smem()] + [vmem()] * 3 + [anywhere()] * 14,
        "attend",
        [
            pltpu.VMEM((4, width, width), BF16),
            pltpu.VMEM(((tile_devices + 2) * block, width), F32),
            pltpu.SemaphoreType.DMA((7 * fsdp,)),
        ],
    )(tile_count, sums, key_gain[None, :], own_tiles, *weights, *mates, *near, *far)
    return attended[None]


def solution(mesh):
    placed = (
        P("fsdp", "tile", None),
        P("fsdp", "tile", None),
        P("fsdp", "tile", None),
        P("fsdp"),
        P("fsdp", None),
        P("fsdp", None),
        P("fsdp", None),
        P("fsdp", None),
        P(),
    )
    return jax.shard_map(
        body, mesh=mesh, in_specs=placed, out_specs=P("fsdp", "tile", None), check_vma=False
    )
```

```python
import functools

import jax
import jax.numpy as jnp
from jax import lax
from jax.experimental import pallas as pl
from jax.experimental.pallas import tpu as pltpu
from jax.sharding import PartitionSpec as P

HEADS = 16
NB = 4
REGIONS_PER_KEY = 8
KEY_DILATION = 2
LANE_GROUPS = 2
STACK_ROWS = 48
F32 = jnp.float32
BF16 = jnp.bfloat16


def vmem():
    return pl.BlockSpec(memory_space=pltpu.VMEM)


def smem():
    return pl.BlockSpec(memory_space=pltpu.SMEM)


def anywhere():
    return pl.BlockSpec(memory_space=pl.ANY)


def hbm():
    return pl.BlockSpec(memory_space=pltpu.HBM)


def over(left, right, left_dim, right_dim, precision=None):
    return lax.dot_general(
        left,
        right,
        (((left_dim,), (right_dim,)), ((), ())),
        precision=precision,
        preferred_element_type=F32,
    )


def pool_kernel(regions, here, mate, other, tiles, out):
    count = tiles.shape[0]
    base = lax.axis_index("tile") * count + 1
    row = lax.broadcasted_iota(jnp.int32, (regions, count), 1) + base
    hits, shares = [], []
    for slots in (here, mate, other):
        turned = slots[...].T
        hit = jnp.zeros((regions, count), F32)
        live = jnp.zeros((regions, 1), F32)
        for s in range(NB):
            slot = turned[:regions, s : s + 1]
            hit += (slot == row).astype(F32)
            live += (slot > 0).astype(F32)
        hits.append(hit.astype(BF16))
        shares.append(1.0 / (jnp.maximum(live, 1.0) * REGIONS_PER_KEY))
    sums = over(jnp.concatenate(hits, axis=0), tiles[...], 1, 0)
    sums = sums * jnp.concatenate(shares, axis=0)
    out[...] = jnp.sum(sums.reshape(-1, REGIONS_PER_KEY, sums.shape[1]), axis=1)


def pair_kernel(mine, theirs, out):
    block = mine.shape[0] // 3
    first = mine[:block] + theirs[block : 2 * block]
    second = mine[block : 2 * block] + theirs[:block]
    inner = jnp.concatenate([first, second], axis=0)
    high = inner.astype(BF16)
    out[: 2 * block, :] = high
    out[2 * block : 4 * block, :] = (inner - high.astype(F32)).astype(BF16)
    outer = jnp.concatenate([mine[2 * block :], theirs[2 * block :]], axis=0)
    out[4 * block :, :] = outer.astype(BF16)


def collect(copies, sem):
    started = []
    for n, (src, dst) in enumerate(copies):
        copy = pltpu.make_async_copy(src, dst, sem.at[n])
        copy.start()
        started.append(copy)
    return started


def sorted_rows(normed):
    keys = normed.shape[0]
    half = keys // KEY_DILATION
    row = lax.broadcasted_iota(jnp.int32, (keys, keys), 0)
    column = lax.broadcasted_iota(jnp.int32, (keys, keys), 1)
    wanted = KEY_DILATION * (row % half) + row // half
    return over((column == wanted).astype(BF16), normed, 1, 0).astype(BF16)


def spread(rows, group, wide):
    half = rows.shape[0] // KEY_DILATION
    heads = HEADS // LANE_GROUPS
    size = wide // heads
    part = rows[:, group * wide : (group + 1) * wide].astype(F32)
    lane = lax.broadcasted_iota(jnp.int32, (half, wide), 1)
    out = []
    for head in range(heads):
        parity = head % KEY_DILATION
        mine = (lane >= head * size) & (lane < (head + 1) * size)
        out.append(jnp.where(mine, part[parity * half : (parity + 1) * half], 0.0))
    return jnp.concatenate(out, axis=0).astype(BF16)


def place_rows(fsdp, shard, held):
    half_width = held.shape[2] // 2
    chips = fsdp // 2
    me = lax.axis_index("fsdp")
    chip, core = me // 2, me % 2

    def at(weight, owner, side):
        rows = pl.ds(pl.multiple_of(owner * shard, shard), shard)
        if side is None:
            return held.at[weight, rows]
        columns = pl.ds(pl.multiple_of(side * half_width, half_width), half_width)
        return held.at[weight, rows, columns]

    def own(weight, piece, mate):
        return [(piece, at(weight, me, None)), (mate, at(weight, 2 * chip + 1 - core, None))]

    def others(weight, near, far, columns=None):
        copies = []
        for j in range(1, chips):
            source = 2 * lax.rem(chip - j + chips, chips)
            copies.append((near(j - 1), at(weight, source + core, columns)))
            copies.append((far(j - 1), at(weight, source + 1 - core, columns)))
        return copies

    return own, others


def attend_kernel(fsdp, block, *refs):
    count, sums, gain, tiles = refs[:4]
    pieces, mates = refs[4:8], refs[8:12]
    near, far = refs[12:15], refs[15:18]
    out, held, pooled, sem = refs[18:]
    device = lax.axis_index("tile")
    cut = device % 2
    own, others = place_rows(fsdp, pieces[0].shape[0], held)

    def from_others(weight, piece, part, columns):
        return others(
            weight, lambda j: near[piece].at[j, part], lambda j: far[piece].at[j, part], columns
        )

    copies, ends = [], []
    for weight in range(4):
        copies += own(weight, pieces[weight], mates[weight])
        if weight == 0:
            copies += from_others(0, 0, 0, 0) + from_others(0, 0, 1, 1)
        elif weight == 1:
            copies += others(1, lambda j: near[1].at[j], lambda j: far[1].at[j])
        else:
            copies += from_others(weight, 0, weight, cut)
            copies += from_others(weight, 2, weight - 2, 1 - cut)
        ends.append(len(copies))
    started = collect(copies, sem)

    def arrive(weight):
        for copy in started[(ends[weight - 1] if weight else 0) : ends[weight]]:
            copy.wait()

    arrive(0)
    query = over(tiles[...], held[0], 1, 0).astype(BF16)
    pooled[...] = jnp.zeros_like(pooled)
    pairs = sums.shape[0] // (6 * block)
    for s in range(pairs):
        even = device ^ (2 * s)
        odd = even ^ 1
        blocks = [even, odd, even, odd, even - 1 + 2 * (even % 2), odd - 1 + 2 * (odd % 2)]
        for i, index in enumerate(blocks):
            begin = (6 * s + i) * block
            rows = pl.ds(pl.multiple_of((index + 1) * block, block), block)
            pooled[rows, :] += sums[begin : begin + block, :].astype(F32)
    mean = pooled[block : (2 * pairs + 1) * block, :]
    scale = lax.rsqrt(jnp.mean(mean * mean, axis=1, keepdims=True) + 1e-06)
    normed = (mean * scale * gain[...]).astype(BF16)
    ordered = sorted_rows(normed)
    arrive(1)
    keys = over(ordered, held[1], 1, 0).astype(BF16)
    arrive(2)
    values = over(ordered, held[2], 1, 0).astype(BF16)
    half = keys.shape[0] // KEY_DILATION
    heads = HEADS // LANE_GROUPS
    wide = keys.shape[1] // LANE_GROUPS
    rows = query.shape[0]
    size = wide // heads
    row = lax.broadcasted_iota(jnp.int32, (half, 1), 0)
    valid = [
        (KEY_DILATION * row + parity) * (4 * REGIONS_PER_KEY) < count[0]
        for parity in range(KEY_DILATION)
    ]
    hidden = jnp.concatenate(
        [jnp.where(valid[head % KEY_DILATION], 0.0, -jnp.inf) for head in range(heads)], axis=0
    )
    contexts = []
    for group in range(LANE_GROUPS):
        lanes = slice(group * wide, (group + 1) * wide)
        score = over(spread(keys, group, wide), query[:, lanes], 1, 1)
        score = (score * (1.0 / size**0.5) + hidden).reshape(heads, half, rows)
        expo = jnp.exp(score - jnp.max(score, axis=1, keepdims=True))
        share = 1.0 / jnp.sum(expo, axis=1, keepdims=True)
        weight = expo.reshape(heads * half, rows).astype(BF16)
        context = over(spread(values, group, wide), weight, 0, 0).reshape(heads, size, rows)
        contexts.append((context * share).reshape(wide, rows).astype(BF16))
    arrive(3)
    context = jnp.concatenate(contexts, axis=0)
    out[...] = over(context, held[3], 0, 0).astype(out.dtype)


def swap(array, axis, offset):
    count = lax.axis_size(axis)
    return lax.ppermute(array, axis, [(i, i ^ offset) for i in range(count)])


def chip_shift(array, axis, step):
    count = lax.axis_size(axis)
    return lax.ppermute(array, axis, [(i, (i + 2 * step) % count) for i in range(count)])


def stack_kernel(w_query, w_value, w_out, stack, sem):
    cut = lax.axis_index("tile") % 2
    width = stack.shape[2]
    halves = ((w_query, 0), (w_query, 1), (w_value, cut), (w_out, cut))
    copies = []
    for n, (w, half) in enumerate(halves):
        columns = pl.ds(pl.multiple_of(half * width, width), width)
        for begin in range(0, w.shape[0], STACK_ROWS):
            part = pl.ds(begin, STACK_ROWS)
            copies.append((w.at[part, columns], stack.at[n, part]))
    for copy in collect(copies, sem):
        copy.wait()


def behind(array, *others):
    return lax.optimization_barrier((array,) + others)[0]


def from_chips(weight):
    chips = lax.axis_size("fsdp") // 2
    return jnp.stack([chip_shift(weight, "fsdp", j) for j in range(1, chips)])


def gather_pairs(rows, axis):
    pairs = lax.axis_size(axis) // 2
    held = 1
    while held < pairs:
        width = min(4, pairs // held)
        parts = [rows] + [swap(rows, axis, 2 * held * d) for d in range(1, width)]
        rows = jnp.concatenate(parts, axis=0)
        held *= width
    return rows


def local_call(kernel, out_shape, in_specs, name, scratch=()):
    return pl.pallas_call(
        kernel,
        out_shape=out_shape,
        in_specs=in_specs,
        out_specs=vmem(),
        scratch_shapes=list(scratch),
        compiler_params=pltpu.CompilerParams(vmem_limit_bytes=40 * 1024 * 1024),
        cost_estimate=pl.CostEstimate(flops=1000, bytes_accessed=1000, transcendentals=0),
        name=name,
    )


def body(tiles, nbr_tiles, nbr_mask, tile_count, w_query, w_key, w_value, w_out, key_gain):
    own_tiles = tiles[0]
    rows, width = own_tiles.shape
    tile_devices = lax.axis_size("tile")
    fsdp = lax.axis_size("fsdp")
    regions = nbr_tiles.shape[1]
    block = regions // REGIONS_PER_KEY

    shard = w_query.shape[0]
    stack = pl.pallas_call(
        stack_kernel,
        out_shape=jax.ShapeDtypeStruct((4, shard, width // 2), BF16),
        in_specs=[hbm()] * 3,
        out_specs=vmem(),
        scratch_shapes=[pltpu.SemaphoreType.DMA((4 * shard // STACK_ROWS,))],
        name="stack",
    )(w_query, w_value, w_out)
    near_stack = from_chips(stack)
    near_key = from_chips(w_key)
    slots = jnp.where(nbr_mask[0].T > 0, nbr_tiles[0].T + 1, 0)
    slots = jnp.pad(slots, ((0, 8 - NB), (0, -regions % 128)))
    mate = swap(slots, "tile", 1)
    inner = [(i, (i + 1) % tile_devices) for i in range(1, tile_devices, 2)]
    other = lax.ppermute(slots, "tile", inner + [(b, a) for a, b in inner])
    mates = [swap(behind(w, slots), "fsdp", 1) for w in (w_query, w_key)]
    mine = local_call(
        functools.partial(pool_kernel, regions),
        jax.ShapeDtypeStruct((3 * block, width), F32),
        [vmem()] * 4,
        "pool",
    )(slots, mate, other, behind(own_tiles, *mates))
    pair = local_call(
        pair_kernel,
        jax.ShapeDtypeStruct((6 * block, width), BF16),
        [vmem()] * 2,
        "pair",
    )(mine, swap(mine, "tile", 1))
    near_stack = behind(near_stack, pair)
    other_halves = swap(near_stack[:, 2:], "tile", 1)
    sums = gather_pairs(pair, "tile")
    far_stack = swap(behind(near_stack, sums), "fsdp", 1)
    mates += [swap(behind(w, sums), "fsdp", 1) for w in (w_value, w_out)]
    near_key = behind(near_key, sums)
    other_halves = behind(other_halves, sums)
    weights = (w_query, w_key, w_value, w_out)
    near = (near_stack, near_key, other_halves)
    far = (far_stack, swap(near_key, "fsdp", 1), swap(other_halves, "fsdp", 1))
    attended = local_call(
        functools.partial(attend_kernel, fsdp, block),
        jax.ShapeDtypeStruct((rows, width), BF16),
        [smem()] + [vmem()] * 3 + [anywhere()] * 14,
        "attend",
        [
            pltpu.VMEM((4, width, width), BF16),
            pltpu.VMEM(((tile_devices + 2) * block, width), F32),
            pltpu.SemaphoreType.DMA((7 * fsdp,)),
        ],
    )(tile_count, sums, key_gain[None, :], own_tiles, *weights, *mates, *near, *far)
    return attended[None]


def solution(mesh):
    placed = (
        P("fsdp", "tile", None),
        P("fsdp", "tile", None),
        P("fsdp", "tile", None),
        P("fsdp"),
        P("fsdp", None),
        P("fsdp", None),
        P("fsdp", None),
        P("fsdp", None),
        P(),
    )
    return jax.shard_map(
        body, mesh=mesh, in_specs=placed, out_specs=P("fsdp", "tile", None), check_vma=False
    )
```

```python
import functools

import jax
import jax.numpy as jnp
from jax import lax
from jax.experimental import pallas as pl
from jax.experimental.pallas import tpu as pltpu
from jax.sharding import PartitionSpec as P

HEADS = 16
NB = 4
REGIONS_PER_KEY = 8
KEY_DILATION = 2
LANE_GROUPS = 2
OUT_PARTS = 2
F32 = jnp.float32
BF16 = jnp.bfloat16


def vmem():
    return pl.BlockSpec(memory_space=pltpu.VMEM)


def smem():
    return pl.BlockSpec(memory_space=pltpu.SMEM)


def anywhere():
    return pl.BlockSpec(memory_space=pl.ANY)


def hbm():
    return pl.BlockSpec(memory_space=pltpu.HBM)


def over(left, right, left_dim, right_dim, precision=None):
    return lax.dot_general(
        left,
        right,
        (((left_dim,), (right_dim,)), ((), ())),
        precision=precision,
        preferred_element_type=F32,
    )


def pool_kernel(regions, here, mate, other, tiles, out):
    count = tiles.shape[0]
    base = lax.axis_index("tile") * count + 1
    row = lax.broadcasted_iota(jnp.int32, (regions, count), 1) + base
    hits, shares = [], []
    for slots in (here, mate, other):
        turned = slots[...].T
        hit = jnp.zeros((regions, count), F32)
        live = jnp.zeros((regions, 1), F32)
        for s in range(NB):
            slot = turned[:regions, s : s + 1]
            hit += (slot == row).astype(F32)
            live += (slot > 0).astype(F32)
        hits.append(hit.astype(BF16))
        shares.append(1.0 / (jnp.maximum(live, 1.0) * REGIONS_PER_KEY))
    sums = over(jnp.concatenate(hits, axis=0), tiles[...], 1, 0)
    sums = sums * jnp.concatenate(shares, axis=0)
    out[...] = jnp.sum(sums.reshape(-1, REGIONS_PER_KEY, sums.shape[1]), axis=1)


def pair_kernel(mine, theirs, out):
    block = mine.shape[0] // 3
    first = mine[:block] + theirs[block : 2 * block]
    second = mine[block : 2 * block] + theirs[:block]
    inner = jnp.concatenate([first, second], axis=0)
    high = inner.astype(BF16)
    out[: 2 * block, :] = high
    out[2 * block : 4 * block, :] = (inner - high.astype(F32)).astype(BF16)
    outer = jnp.concatenate([mine[2 * block :], theirs[2 * block :]], axis=0)
    out[4 * block :, :] = outer.astype(BF16)


def collect(copies, sem):
    started = []
    for n, (src, dst) in enumerate(copies):
        copy = pltpu.make_async_copy(src, dst, sem.at[n])
        copy.start()
        started.append(copy)
    return started


def sorted_rows(normed):
    keys = normed.shape[0]
    half = keys // KEY_DILATION
    row = lax.broadcasted_iota(jnp.int32, (keys, keys), 0)
    column = lax.broadcasted_iota(jnp.int32, (keys, keys), 1)
    wanted = KEY_DILATION * (row % half) + row // half
    return over((column == wanted).astype(BF16), normed, 1, 0).astype(BF16)


def spread(rows, group, wide):
    half = rows.shape[0] // KEY_DILATION
    heads = HEADS // LANE_GROUPS
    size = wide // heads
    part = rows[:, group * wide : (group + 1) * wide].astype(F32)
    lane = lax.broadcasted_iota(jnp.int32, (half, wide), 1)
    out = []
    for head in range(heads):
        parity = head % KEY_DILATION
        mine = (lane >= head * size) & (lane < (head + 1) * size)
        out.append(jnp.where(mine, part[parity * half : (parity + 1) * half], 0.0))
    return jnp.concatenate(out, axis=0).astype(BF16)


def place_rows(fsdp, shard, held):
    half_width = held.shape[2] // 2
    chips = fsdp // 2
    me = lax.axis_index("fsdp")
    chip, core = me // 2, me % 2

    def at(weight, owner, side):
        rows = pl.ds(pl.multiple_of(owner * shard, shard), shard)
        if side is None:
            return held.at[weight, rows]
        columns = pl.ds(pl.multiple_of(side * half_width, half_width), half_width)
        return held.at[weight, rows, columns]

    def own(weight, piece, mate):
        return [(piece, at(weight, me, None)), (mate, at(weight, 2 * chip + 1 - core, None))]

    def others(weight, near, far, columns=None):
        copies = []
        for j in range(1, chips):
            source = 2 * lax.rem(chip - j + chips, chips)
            copies.append((near(j - 1), at(weight, source + core, columns)))
            copies.append((far(j - 1), at(weight, source + 1 - core, columns)))
        return copies

    return own, others


def attend_kernel(fsdp, block, *refs):
    count, sums, gain, tiles = refs[:4]
    pieces, mates = refs[4:8], refs[8:12]
    near, far = refs[12:15], refs[15:18]
    out, held, pooled, made, sem, out_sem = refs[18:]
    device = lax.axis_index("tile")
    cut = device % 2
    own, others = place_rows(fsdp, pieces[0].shape[0], held)

    def from_others(weight, piece, part, columns):
        return others(
            weight, lambda j: near[piece].at[j, part], lambda j: far[piece].at[j, part], columns
        )

    copies, ends = [], []
    for weight in range(4):
        copies += own(weight, pieces[weight], mates[weight])
        if weight == 0:
            copies += from_others(0, 0, 0, 0) + from_others(0, 0, 1, 1)
        elif weight == 1:
            copies += others(1, lambda j: near[1].at[j], lambda j: far[1].at[j])
        else:
            copies += from_others(weight, 0, weight, cut)
            copies += from_others(weight, 2, weight - 2, 1 - cut)
        ends.append(len(copies))
    started = collect(copies, sem)

    def arrive(weight):
        for copy in started[(ends[weight - 1] if weight else 0) : ends[weight]]:
            copy.wait()

    arrive(0)
    query = over(tiles[...], held[0], 1, 0).astype(BF16)
    pooled[...] = jnp.zeros_like(pooled)
    pairs = sums.shape[0] // (6 * block)
    for s in range(pairs):
        even = device ^ (2 * s)
        odd = even ^ 1
        blocks = [even, odd, even, odd, even - 1 + 2 * (even % 2), odd - 1 + 2 * (odd % 2)]
        for i, index in enumerate(blocks):
            begin = (6 * s + i) * block
            rows = pl.ds(pl.multiple_of((index + 1) * block, block), block)
            pooled[rows, :] += sums[begin : begin + block, :].astype(F32)
    mean = pooled[block : (2 * pairs + 1) * block, :]
    scale = lax.rsqrt(jnp.mean(mean * mean, axis=1, keepdims=True) + 1e-06)
    normed = (mean * scale * gain[...]).astype(BF16)
    ordered = sorted_rows(normed)
    for weight in range(1, 4):
        arrive(weight)
    keys = over(ordered, held[1], 1, 0).astype(BF16)
    values = over(ordered, held[2], 1, 0).astype(BF16)
    half = keys.shape[0] // KEY_DILATION
    heads = HEADS // LANE_GROUPS
    wide = keys.shape[1] // LANE_GROUPS
    rows = query.shape[0]
    size = wide // heads
    row = lax.broadcasted_iota(jnp.int32, (half, 1), 0)
    valid = [
        (KEY_DILATION * row + parity) * (4 * REGIONS_PER_KEY) < count[0]
        for parity in range(KEY_DILATION)
    ]
    hidden = jnp.concatenate(
        [jnp.where(valid[head % KEY_DILATION], 0.0, -jnp.inf) for head in range(heads)], axis=0
    )
    contexts = []
    for group in range(LANE_GROUPS):
        lanes = slice(group * wide, (group + 1) * wide)
        score = over(spread(keys, group, wide), query[:, lanes], 1, 1)
        score = (score * (1.0 / size**0.5) + hidden).reshape(heads, half, rows)
        expo = jnp.exp(score - jnp.max(score, axis=1, keepdims=True))
        share = 1.0 / jnp.sum(expo, axis=1, keepdims=True)
        weight = expo.reshape(heads * half, rows).astype(BF16)
        context = over(spread(values, group, wide), weight, 0, 0).reshape(heads, size, rows)
        contexts.append((context * share).reshape(wide, rows).astype(BF16))
    context = jnp.concatenate(contexts, axis=0)
    leaving = []
    for part in range(OUT_PARTS):
        piece = pl.ds(part * rows // OUT_PARTS, rows // OUT_PARTS)
        lanes = slice(part * rows // OUT_PARTS, (part + 1) * rows // OUT_PARTS)
        made[piece, :] = over(context[:, lanes], held[3], 0, 0).astype(made.dtype)
        copy = pltpu.make_async_copy(made.at[piece], out.at[piece], out_sem.at[part])
        copy.start()
        leaving.append(copy)
    for copy in leaving:
        copy.wait()


def swap(array, axis, offset):
    count = lax.axis_size(axis)
    return lax.ppermute(array, axis, [(i, i ^ offset) for i in range(count)])


def chip_shift(array, axis, step):
    count = lax.axis_size(axis)
    return lax.ppermute(array, axis, [(i, (i + 2 * step) % count) for i in range(count)])


def stack_kernel(w_query, w_value, w_out, stack, sem):
    cut = lax.axis_index("tile") % 2
    width = stack.shape[2]
    halves = ((w_query, 0), (w_query, 1), (w_value, cut), (w_out, cut))
    copies = []
    for n, (w, half) in enumerate(halves):
        columns = pl.ds(pl.multiple_of(half * width, width), width)
        copies.append((w.at[:, columns], stack.at[n]))
    for copy in collect(copies, sem):
        copy.wait()


def behind(array, *others):
    return lax.optimization_barrier((array,) + others)[0]


def from_chips(weight):
    chips = lax.axis_size("fsdp") // 2
    return jnp.stack([chip_shift(weight, "fsdp", j) for j in range(1, chips)])


def gather_pairs(rows, axis):
    pairs = lax.axis_size(axis) // 2
    held = 1
    while held < pairs:
        width = min(4, pairs // held)
        parts = [rows] + [swap(rows, axis, 2 * held * d) for d in range(1, width)]
        rows = jnp.concatenate(parts, axis=0)
        held *= width
    return rows


def local_call(kernel, out_shape, in_specs, name, scratch=(), out_spec=None):
    return pl.pallas_call(
        kernel,
        out_shape=out_shape,
        in_specs=in_specs,
        out_specs=vmem() if out_spec is None else out_spec,
        scratch_shapes=list(scratch),
        compiler_params=pltpu.CompilerParams(vmem_limit_bytes=40 * 1024 * 1024),
        cost_estimate=pl.CostEstimate(flops=1000, bytes_accessed=1000, transcendentals=0),
        name=name,
    )


def body(tiles, nbr_tiles, nbr_mask, tile_count, w_query, w_key, w_value, w_out, key_gain):
    own_tiles = tiles[0]
    rows, width = own_tiles.shape
    tile_devices = lax.axis_size("tile")
    fsdp = lax.axis_size("fsdp")
    regions = nbr_tiles.shape[1]
    block = regions // REGIONS_PER_KEY

    shard = w_query.shape[0]
    stack = pl.pallas_call(
        stack_kernel,
        out_shape=jax.ShapeDtypeStruct((4, shard, width // 2), BF16),
        in_specs=[hbm()] * 3,
        out_specs=vmem(),
        scratch_shapes=[pltpu.SemaphoreType.DMA((4,))],
        name="stack",
    )(w_query, w_value, w_out)
    near_stack = from_chips(stack)
    near_key = from_chips(w_key)
    slots = jnp.where(nbr_mask[0].T > 0, nbr_tiles[0].T + 1, 0)
    slots = jnp.pad(slots, ((0, 8 - NB), (0, -regions % 128)))
    mate = swap(slots, "tile", 1)
    inner = [(i, i + 1) for i in range(1, tile_devices - 1, 2)]
    other = lax.ppermute(slots, "tile", inner + [(b, a) for a, b in inner])
    mates = [swap(behind(w, slots), "fsdp", 1) for w in (w_query, w_key)]
    mine = local_call(
        functools.partial(pool_kernel, regions),
        jax.ShapeDtypeStruct((3 * block, width), F32),
        [vmem()] * 4,
        "pool",
    )(slots, mate, other, behind(own_tiles, *mates))
    pair = local_call(
        pair_kernel,
        jax.ShapeDtypeStruct((6 * block, width), BF16),
        [vmem()] * 2,
        "pair",
    )(mine, swap(mine, "tile", 1))
    near_stack = behind(near_stack, pair)
    other_halves = swap(near_stack[:, 2:], "tile", 1)
    sums = gather_pairs(pair, "tile")
    far_stack = swap(behind(near_stack, sums), "fsdp", 1)
    mates += [swap(behind(w, sums), "fsdp", 1) for w in (w_value, w_out)]
    near_key = behind(near_key, sums)
    other_halves = behind(other_halves, sums)
    weights = (w_query, w_key, w_value, w_out)
    near = (near_stack, near_key, other_halves)
    far = (far_stack, swap(near_key, "fsdp", 1), swap(other_halves, "fsdp", 1))
    attended = local_call(
        functools.partial(attend_kernel, fsdp, block),
        jax.ShapeDtypeStruct((rows, width), BF16),
        [smem()] + [vmem()] * 3 + [anywhere()] * 14,
        "attend",
        [
            pltpu.VMEM((4, width, width), BF16),
            pltpu.VMEM(((tile_devices + 2) * block, width), F32),
            pltpu.VMEM((rows, width), BF16),
            pltpu.SemaphoreType.DMA((7 * fsdp,)),
            pltpu.SemaphoreType.DMA((OUT_PARTS,)),
        ],
        hbm(),
    )(tile_count, sums, key_gain[None, :], own_tiles, *weights, *mates, *near, *far)
    return attended[None]


def solution(mesh):
    placed = (
        P("fsdp", "tile", None),
        P("fsdp", "tile", None),
        P("fsdp", "tile", None),
        P("fsdp"),
        P("fsdp", None),
        P("fsdp", None),
        P("fsdp", None),
        P("fsdp", None),
        P(),
    )
    return jax.shard_map(
        body, mesh=mesh, in_specs=placed, out_specs=P("fsdp", "tile", None), check_vma=False
    )
```

```python
import functools

import jax
import jax.numpy as jnp
from jax import lax
from jax.experimental import pallas as pl
from jax.experimental.pallas import tpu as pltpu
from jax.sharding import PartitionSpec as P

HEADS = 16
NB = 4
REGIONS_PER_KEY = 8
KEY_DILATION = 2
LANE_GROUPS = 2
OUT_PARTS = 2
F32 = jnp.float32
BF16 = jnp.bfloat16


def vmem():
    return pl.BlockSpec(memory_space=pltpu.VMEM)


def smem():
    return pl.BlockSpec(memory_space=pltpu.SMEM)


def anywhere():
    return pl.BlockSpec(memory_space=pl.ANY)


def hbm():
    return pl.BlockSpec(memory_space=pltpu.HBM)


def over(left, right, left_dim, right_dim, precision=None):
    return lax.dot_general(
        left,
        right,
        (((left_dim,), (right_dim,)), ((), ())),
        precision=precision,
        preferred_element_type=F32,
    )


def pool_kernel(regions, here, mate, other, tiles, out):
    count = tiles.shape[0]
    base = lax.axis_index("tile") * count + 1
    row = lax.broadcasted_iota(jnp.int32, (regions, count), 1) + base
    hits, shares = [], []
    for slots in (here, mate, other):
        turned = slots[...].T
        hit = jnp.zeros((regions, count), F32)
        live = jnp.zeros((regions, 1), F32)
        for s in range(NB):
            slot = turned[:regions, s : s + 1]
            hit += (slot == row).astype(F32)
            live += (slot > 0).astype(F32)
        hits.append(hit.astype(BF16))
        shares.append(1.0 / (jnp.maximum(live, 1.0) * REGIONS_PER_KEY))
    sums = over(jnp.concatenate(hits, axis=0), tiles[...], 1, 0)
    sums = sums * jnp.concatenate(shares, axis=0)
    out[...] = jnp.sum(sums.reshape(-1, REGIONS_PER_KEY, sums.shape[1]), axis=1)


def pair_kernel(mine, theirs, out):
    block = mine.shape[0] // 3
    first = mine[:block] + theirs[block : 2 * block]
    second = mine[block : 2 * block] + theirs[:block]
    inner = jnp.concatenate([first, second], axis=0)
    high = inner.astype(BF16)
    out[: 2 * block, :] = high
    out[2 * block : 4 * block, :] = (inner - high.astype(F32)).astype(BF16)
    outer = jnp.concatenate([mine[2 * block :], theirs[2 * block :]], axis=0)
    out[4 * block :, :] = outer.astype(BF16)


def collect(copies, sem):
    started = []
    for n, (src, dst) in enumerate(copies):
        copy = pltpu.make_async_copy(src, dst, sem.at[n])
        copy.start()
        started.append(copy)
    return started


def sorted_rows(normed):
    keys = normed.shape[0]
    half = keys // KEY_DILATION
    row = lax.broadcasted_iota(jnp.int32, (keys, keys), 0)
    column = lax.broadcasted_iota(jnp.int32, (keys, keys), 1)
    wanted = KEY_DILATION * (row % half) + row // half
    return over((column == wanted).astype(BF16), normed, 1, 0).astype(BF16)


def spread(rows, group, wide):
    half = rows.shape[0] // KEY_DILATION
    heads = HEADS // LANE_GROUPS
    size = wide // heads
    part = rows[:, group * wide : (group + 1) * wide].astype(F32)
    lane = lax.broadcasted_iota(jnp.int32, (half, wide), 1)
    out = []
    for head in range(heads):
        parity = head % KEY_DILATION
        mine = (lane >= head * size) & (lane < (head + 1) * size)
        out.append(jnp.where(mine, part[parity * half : (parity + 1) * half], 0.0))
    return jnp.concatenate(out, axis=0).astype(BF16)


def place_rows(fsdp, shard, held):
    half_width = held.shape[2] // 2
    chips = fsdp // 2
    me = lax.axis_index("fsdp")
    chip, core = me // 2, me % 2

    def at(weight, owner, side):
        rows = pl.ds(pl.multiple_of(owner * shard, shard), shard)
        if side is None:
            return held.at[weight, rows]
        columns = pl.ds(pl.multiple_of(side * half_width, half_width), half_width)
        return held.at[weight, rows, columns]

    def own(weight, piece, mate):
        return [(piece, at(weight, me, None)), (mate, at(weight, 2 * chip + 1 - core, None))]

    def others(weight, near, far, columns=None):
        copies = []
        for j in range(1, chips):
            source = 2 * lax.rem(chip - j + chips, chips)
            copies.append((near(j - 1), at(weight, source + core, columns)))
            copies.append((far(j - 1), at(weight, source + 1 - core, columns)))
        return copies

    return own, others


def attend_kernel(fsdp, block, *refs):
    count, sums, gain, tiles = refs[:4]
    pieces, mates = refs[4:8], refs[8:12]
    near, far = refs[12:15], refs[15:18]
    out, held, pooled, made, sem, out_sem = refs[18:]
    device = lax.axis_index("tile")
    cut = device % 2
    own, others = place_rows(fsdp, pieces[0].shape[0], held)

    def from_others(weight, piece, part, columns):
        return others(
            weight, lambda j: near[piece].at[j, part], lambda j: far[piece].at[j, part], columns
        )

    copies, ends = [], []
    for weight in range(4):
        copies += own(weight, pieces[weight], mates[weight])
        if weight == 0:
            copies += from_others(0, 0, 0, 0) + from_others(0, 0, 1, 1)
        elif weight == 1:
            copies += others(1, lambda j: near[1].at[j], lambda j: far[1].at[j])
        else:
            copies += from_others(weight, 0, weight, cut)
            copies += from_others(weight, 2, weight - 2, 1 - cut)
        ends.append(len(copies))
    started = collect(copies, sem)

    def arrive(weight):
        for copy in started[(ends[weight - 1] if weight else 0) : ends[weight]]:
            copy.wait()

    pooled[...] = jnp.zeros_like(pooled)
    pairs = sums.shape[0] // (6 * block)
    for s in range(pairs):
        even = device ^ (2 * s)
        odd = even ^ 1
        blocks = [even, odd, even, odd, even - 1 + 2 * (even % 2), odd - 1 + 2 * (odd % 2)]
        for i, index in enumerate(blocks):
            begin = (6 * s + i) * block
            rows = pl.ds(pl.multiple_of((index + 1) * block, block), block)
            pooled[rows, :] += sums[begin : begin + block, :].astype(F32)
    mean = pooled[block : (2 * pairs + 1) * block, :]
    scale = lax.rsqrt(jnp.mean(mean * mean, axis=1, keepdims=True) + 1e-06)
    normed = (mean * scale * gain[...]).astype(BF16)
    ordered = sorted_rows(normed)
    for weight in range(4):
        arrive(weight)
    query = over(tiles[...], held[0], 1, 0).astype(BF16)
    keys = over(ordered, held[1], 1, 0).astype(BF16)
    values = over(ordered, held[2], 1, 0).astype(BF16)
    half = keys.shape[0] // KEY_DILATION
    heads = HEADS // LANE_GROUPS
    wide = keys.shape[1] // LANE_GROUPS
    rows = query.shape[0]
    size = wide // heads
    row = lax.broadcasted_iota(jnp.int32, (half, 1), 0)
    valid = [
        (KEY_DILATION * row + parity) * (4 * REGIONS_PER_KEY) < count[0]
        for parity in range(KEY_DILATION)
    ]
    hidden = jnp.concatenate(
        [jnp.where(valid[head % KEY_DILATION], 0.0, -jnp.inf) for head in range(heads)], axis=0
    )
    contexts = []
    for group in range(LANE_GROUPS):
        lanes = slice(group * wide, (group + 1) * wide)
        score = over(spread(keys, group, wide), query[:, lanes], 1, 1)
        score = (score * (1.0 / size**0.5) + hidden).reshape(heads, half, rows)
        expo = jnp.exp(score - jnp.max(score, axis=1, keepdims=True))
        share = 1.0 / jnp.sum(expo, axis=1, keepdims=True)
        weight = expo.reshape(heads * half, rows).astype(BF16)
        context = over(spread(values, group, wide), weight, 0, 0).reshape(heads, size, rows)
        contexts.append((context * share).reshape(wide, rows).astype(BF16))
    context = jnp.concatenate(contexts, axis=0)
    leaving = []
    for part in range(OUT_PARTS):
        piece = pl.ds(part * rows // OUT_PARTS, rows // OUT_PARTS)
        lanes = slice(part * rows // OUT_PARTS, (part + 1) * rows // OUT_PARTS)
        made[piece, :] = over(context[:, lanes], held[3], 0, 0).astype(made.dtype)
        copy = pltpu.make_async_copy(made.at[piece], out.at[piece], out_sem.at[part])
        copy.start()
        leaving.append(copy)
    for copy in leaving:
        copy.wait()


def swap(array, axis, offset):
    count = lax.axis_size(axis)
    return lax.ppermute(array, axis, [(i, i ^ offset) for i in range(count)])


def chip_shift(array, axis, step):
    count = lax.axis_size(axis)
    return lax.ppermute(array, axis, [(i, (i + 2 * step) % count) for i in range(count)])


def stack_kernel(w_query, w_value, w_out, stack, sem):
    cut = lax.axis_index("tile") % 2
    width = stack.shape[2]
    halves = ((w_query, 0), (w_query, 1), (w_value, cut), (w_out, cut))
    copies = []
    for n, (w, half) in enumerate(halves):
        columns = pl.ds(pl.multiple_of(half * width, width), width)
        copies.append((w.at[:, columns], stack.at[n]))
    for copy in collect(copies, sem):
        copy.wait()


def behind(array, *others):
    return lax.optimization_barrier((array,) + others)[0]


def from_chips(weight):
    chips = lax.axis_size("fsdp") // 2
    return jnp.stack([chip_shift(weight, "fsdp", j) for j in range(1, chips)])


def gather_pairs(rows, axis):
    pairs = lax.axis_size(axis) // 2
    held = 1
    while held < pairs:
        width = min(4, pairs // held)
        parts = [rows] + [swap(rows, axis, 2 * held * d) for d in range(1, width)]
        rows = jnp.concatenate(parts, axis=0)
        held *= width
    return rows


def local_call(kernel, out_shape, in_specs, name, scratch=(), out_spec=None):
    return pl.pallas_call(
        kernel,
        out_shape=out_shape,
        in_specs=in_specs,
        out_specs=vmem() if out_spec is None else out_spec,
        scratch_shapes=list(scratch),
        compiler_params=pltpu.CompilerParams(vmem_limit_bytes=40 * 1024 * 1024),
        cost_estimate=pl.CostEstimate(flops=1000, bytes_accessed=1000, transcendentals=0),
        name=name,
    )


def body(tiles, nbr_tiles, nbr_mask, tile_count, w_query, w_key, w_value, w_out, key_gain):
    own_tiles = tiles[0]
    rows, width = own_tiles.shape
    tile_devices = lax.axis_size("tile")
    fsdp = lax.axis_size("fsdp")
    regions = nbr_tiles.shape[1]
    block = regions // REGIONS_PER_KEY

    shard = w_query.shape[0]
    stack = pl.pallas_call(
        stack_kernel,
        out_shape=jax.ShapeDtypeStruct((4, shard, width // 2), BF16),
        in_specs=[hbm()] * 3,
        out_specs=vmem(),
        scratch_shapes=[pltpu.SemaphoreType.DMA((4,))],
        name="stack",
    )(w_query, w_value, w_out)
    near_stack = from_chips(stack)
    near_key = from_chips(w_key)
    slots = jnp.where(nbr_mask[0].T > 0, nbr_tiles[0].T + 1, 0)
    slots = jnp.pad(slots, ((0, 8 - NB), (0, -regions % 128)))
    mate = swap(slots, "tile", 1)
    inner = [(i, i + 1) for i in range(1, tile_devices - 1, 2)]
    other = lax.ppermute(slots, "tile", inner + [(b, a) for a, b in inner])
    mates = [swap(behind(w, slots), "fsdp", 1) for w in (w_query, w_key)]
    mine = local_call(
        functools.partial(pool_kernel, regions),
        jax.ShapeDtypeStruct((3 * block, width), F32),
        [vmem()] * 4,
        "pool",
    )(slots, mate, other, behind(own_tiles, *mates))
    pair = local_call(
        pair_kernel,
        jax.ShapeDtypeStruct((6 * block, width), BF16),
        [vmem()] * 2,
        "pair",
    )(mine, swap(mine, "tile", 1))
    near_stack = behind(near_stack, pair)
    other_halves = swap(near_stack[:, 2:], "tile", 1)
    sums = gather_pairs(pair, "tile")
    far_stack = swap(behind(near_stack, sums), "fsdp", 1)
    mates += [swap(behind(w, sums), "fsdp", 1) for w in (w_value, w_out)]
    near_key = behind(near_key, sums)
    other_halves = behind(other_halves, sums)
    weights = (w_query, w_key, w_value, w_out)
    near = (near_stack, near_key, other_halves)
    far = (far_stack, swap(near_key, "fsdp", 1), swap(other_halves, "fsdp", 1))
    attended = local_call(
        functools.partial(attend_kernel, fsdp, block),
        jax.ShapeDtypeStruct((rows, width), BF16),
        [smem()] + [vmem()] * 3 + [anywhere()] * 14,
        "attend",
        [
            pltpu.VMEM((4, width, width), BF16),
            pltpu.VMEM(((tile_devices + 2) * block, width), F32),
            pltpu.VMEM((rows, width), BF16),
            pltpu.SemaphoreType.DMA((7 * fsdp,)),
            pltpu.SemaphoreType.DMA((OUT_PARTS,)),
        ],
        hbm(),
    )(tile_count, sums, key_gain[None, :], own_tiles, *weights, *mates, *near, *far)
    return attended[None]


def solution(mesh):
    placed = (
        P("fsdp", "tile", None),
        P("fsdp", "tile", None),
        P("fsdp", "tile", None),
        P("fsdp"),
        P("fsdp", None),
        P("fsdp", None),
        P("fsdp", None),
        P("fsdp", None),
        P(),
    )
    return jax.shard_map(
        body, mesh=mesh, in_specs=placed, out_specs=P("fsdp", "tile", None), check_vma=False
    )
```
